32 devices in a mesh: band: 4 (over y, x), bl: 8 (over z, core).
Axes of the slice: x: 2, y: 2, z: 4, core: 2. Of those that a mesh axis runs over, the one named last changes fastest.
Arguments:
- visibilities: bfloat16 [4096, 8, 2, 1024], P('bl', None, None, 'band'), may hold values from -400 to 400
- send_order: int32 [8, 512], P('bl'), may hold values from 0 to 511, each once within a row
- channel_flags: int32 [1024], replicated, may hold values 0 or 1
- group_ids: int32 [4096], P(('band', 'bl')), may hold values from 0 to 15, as said below
- pair_list: int32 [8192, 2], P(('band', 'bl')), may hold values from 0 to 255, as said below
Outputs:
- group_power: float32 [512, 1024], P(('band', 'bl'))
The draws below stay inside these ranges and needn't reach their ends.
Inputs may be any that keep to these rules, and one draw needn't show every extreme that they name: `send_order`: row j lists each of the 512 baselines of bl block j once; positions d * 16 to (d + 1) * 16 - 1 name those that owner d receives. `group_ids`: among the 128 baselines of one owner, each group id is held by exactly 8 of them. `pair_list`: in each row (i, j) of an owner's 256 pairs, i is a local baseline; j below 128 is a local baseline, j of 128 or more is baseline j - 128 of the owner one step lower along band (cyclically); j != i; every group of the owner has at least one pair whose i lies in it.
All inputs are finite; a program needn't handle non-finite values.
Results may differ from the reference program's by a relative error of at most 0.0065.
Values may be sent and summed in bfloat16 or wider, within the bound.
No kernel may reach another device: no remote copies, remote signals or barrier semaphores. Data moves between devices by JAX's collectives and lax.ppermute only.
A program may use at most 128 MiB of HBM per device.

```python
import math
import jax
import jax.numpy as jnp
from jax import lax

F = 1024
TIMES = 8
BL_DEV = 128
GRP_DEV = 16
PAIRS_DEV = 256
NB = 4096
BLK = 512
NPAIRS = 8192
NGROUPS = 512
N_BAND = 4
N_BL = 8
DEVICES = 32


def draw_visibilities(key, part):
    key_noise, key_rows, key_chans = jax.random.split(key, 3)
    noise_base = jnp.clip(jax.random.normal(key_noise, (NB, TIMES, 2, F), jnp.float32), -4.0, 4.0)
    row_scale = jnp.exp(jax.random.uniform(key_rows, (NB, 1, 1, 1), jnp.float32, 0.0, math.log(10.0)))
    chan_scale = jnp.exp(jax.random.uniform(key_chans, (1, 1, 1, F), jnp.float32, 0.0, math.log(10.0)))
    return (noise_base * row_scale * chan_scale).astype(jnp.bfloat16)


def ownership_tables(key):
    folded = jax.random.fold_in(key, 11)
    device_keys = jax.random.split(folded, DEVICES)

    def one_device(device_key):
        key_perm, key_pick, key_loose, key_partner = jax.random.split(device_key, 4)
        group_size = BL_DEV // GRP_DEV
        order = jax.random.permutation(key_perm, BL_DEV).astype(jnp.int32)
        groups = jnp.zeros((BL_DEV,), jnp.int32).at[order].set(jnp.arange(BL_DEV, dtype=jnp.int32) // group_size)
        pair_slot = jnp.arange(PAIRS_DEV, dtype=jnp.int32)
        member_pick = jax.random.randint(key_pick, (PAIRS_DEV,), 0, group_size, dtype=jnp.int32)
        anchored = order[jnp.minimum(pair_slot, GRP_DEV - 1) * group_size + member_pick]
        scattered = jax.random.randint(key_loose, (PAIRS_DEV,), 0, BL_DEV, dtype=jnp.int32)
        first = jnp.where(pair_slot < GRP_DEV, anchored, scattered)
        offset = jax.random.randint(key_partner, (PAIRS_DEV,), 0, 2 * BL_DEV - 1, dtype=jnp.int32)
        second = (first + 1 + offset) % (2 * BL_DEV)
        return (groups, jnp.stack([first, second], axis=1))
    groups, pairs = jax.vmap(one_device)(device_keys)
    return (groups.reshape(NB), pairs.reshape(NPAIRS, 2))


def draw_group_ids(key, part):
    return ownership_tables(key)[0]


def draw_pair_list(key, part):
    return ownership_tables(key)[1]


def touch_ends(array, key, smallest, largest):
    longest = array.shape.index(max(array.shape))
    spots = []
    for shift in (0, 1):
        where = [jax.random.randint(jax.random.fold_in(key, axis), (), 0, length) for axis, length in enumerate(array.shape)]
        where[longest] = (where[longest] + shift) % array.shape[longest]
        spots.append(tuple(where))
    return array.at[spots[0]].set(smallest).at[spots[1]].set(largest)


def setup_inputs(seed: int = 0) -> dict:
    key_of = jax.random.split(jax.random.key(seed), 6)
    visibilities = draw_visibilities(jax.random.fold_in(key_of[5], 71), 0)
    send_order = jax.vmap(lambda own: jax.random.permutation(own, BLK))(jax.random.split(key_of[1], N_BL)).reshape((N_BL, BLK)).astype(jnp.int32)
    channel_flags = touch_ends((jax.random.randint(key_of[2], (F,), 0, 8) < 7).astype(jnp.int32), jax.random.fold_in(key_of[2], 1), 0, 1)
    group_ids = draw_group_ids(jax.random.fold_in(key_of[5], 71), 0)
    pair_list = draw_pair_list(jax.random.fold_in(key_of[5], 71), 0)
    return dict(visibilities=visibilities, send_order=send_order, channel_flags=channel_flags, group_ids=group_ids, pair_list=pair_list)


def delay_matrix(full_width):
    index = jnp.arange(full_width, dtype=jnp.int32)
    phase = index[:, None] * index[None, :] % full_width
    angle = phase.astype(jnp.float32) * (2.0 * math.pi / full_width)
    cosine = jnp.cos(angle)
    sine = jnp.sin(angle)
    upper = jnp.concatenate([cosine, -sine], axis=1)
    lower = jnp.concatenate([sine, cosine], axis=1)
    return jnp.concatenate([upper, lower], axis=0).astype(jnp.bfloat16)

def channel_weights(channel_flags):
    width = channel_flags.shape[0]
    angle = jnp.arange(width, dtype=jnp.float32) * (2.0 * math.pi / width)
    taper = 0.35875 - 0.48829 * jnp.cos(angle) + 0.14128 * jnp.cos(2.0 * angle) - 0.01168 * jnp.cos(3.0 * angle)
    return taper * channel_flags.astype(jnp.float32)

def group_spectra(own_rows, previous, pair_list, group_ids):
    window = jnp.concatenate([own_rows, previous], axis=0).astype(jnp.float32)
    slots = window.shape[1] * window.shape[2]
    energy = jnp.einsum('btc,btc->b', window, window) / slots + 1e-06
    first = pair_list[:, 0]
    second = pair_list[:, 1]
    left = jnp.take(window, first, axis=0)
    right = jnp.take(window, second, axis=0)
    product = jnp.einsum('ptc,ptc->pc', left, right)
    half = product.shape[1] // 2
    cross = product[:, :half] + product[:, half:]
    scale = energy[first] * energy[second]
    power = cross / jnp.sqrt(scale)[:, None]
    weight = 1.0 / scale
    member = (group_ids[first][None, :] == jnp.arange(GRP_DEV, dtype=jnp.int32)[:, None]).astype(jnp.float32)
    numer = jnp.dot(member, weight[:, None] * power, precision=lax.Precision.HIGHEST)
    denom = jnp.dot(member, weight, precision=lax.Precision.HIGHEST)
    return numer / denom[:, None]

def reference(visibilities, send_order, channel_flags, group_ids, pair_list):
    device_count = N_BAND * N_BL
    peer_rows = BL_DEV // N_BL
    matrix = delay_matrix(F)
    weights = channel_weights(channel_flags).reshape(2 * 0 + 1, F)
    offsets = (jnp.arange(N_BL, dtype=jnp.int32) * BLK)[None, :, None]
    source = send_order.reshape(N_BL, device_count, peer_rows).transpose(1, 0, 2) + offsets
    source = source.reshape(device_count, BL_DEV).astype(jnp.int32)

    def one_device(rows):
        owned = jnp.take(visibilities, rows, axis=0)
        tapered = (owned.astype(jnp.float32) * weights[None, None, :, :]).astype(jnp.bfloat16)
        tapered = tapered.reshape(BL_DEV * TIMES, 2 * F)
        spectra = jnp.dot(tapered, matrix, preferred_element_type=jnp.float32).astype(jnp.bfloat16)
        return spectra.reshape(BL_DEV, TIMES, 2 * F)
    spectra = lax.map(one_device, source)
    pairs_split = pair_list.reshape(device_count, PAIRS_DEV, 2)
    groups_split = group_ids.reshape(device_count, BL_DEV)

    def one_owner(packed):
        device, pairs_here, groups_here = packed
        band_index = device // N_BL
        bl_index = device % N_BL
        prior_index = (band_index - 1 + N_BAND) % N_BAND * N_BL + bl_index
        own_rows = lax.dynamic_index_in_dim(spectra, device, 0, keepdims=False)
        previous = lax.dynamic_index_in_dim(spectra, prior_index, 0, keepdims=False)
        return group_spectra(own_rows, previous, pairs_here, groups_here)
    result = lax.map(one_owner, (jnp.arange(device_count, dtype=jnp.int32), pairs_split, groups_split))
    return result.reshape(NGROUPS, F)
```

```python
import functools
import math

import jax
import jax.numpy as jnp
import ml_dtypes
import numpy as np
from jax import lax
from jax.experimental import pallas as pl
from jax.experimental.pallas import tpu as pltpu
from jax.sharding import PartitionSpec as P

GRP_DEV = 16
LANES = 128
ENERGY_PARTS = 3
EXTRA_ROWS = 16
HIGHEST = lax.Precision.HIGHEST
VMEM_LIMIT = 20 * 1024 * 1024
F32 = jnp.float32
BF16 = jnp.bfloat16
VMEM = pl.BlockSpec(memory_space=pltpu.VMEM)
SMEM = pl.BlockSpec(memory_space=pltpu.SMEM)


def shifted(value, axis, steps):
    count = lax.axis_size(axis)
    pairs = [(source, (source + steps) % count) for source in range(count)]
    return lax.ppermute(value, axis, pairs)


def spread(pieces):
    return [pieces[0]] + [shifted(pieces[s], "band", s) for s in range(1, len(pieces))]


def cost(flops, bytes_accessed):
    return pl.CostEstimate(flops=flops, bytes_accessed=bytes_accessed, transcendentals=0)


def params():
    return pltpu.CompilerParams(vmem_limit_bytes=VMEM_LIMIT)


def class_matrices(full_width, classes):
    sub = full_width // classes
    channel = np.arange(sub)[None, :, None]
    delay = classes * np.arange(sub)[None, None, :] + np.arange(classes)[:, None, None]
    angle = (channel * delay % full_width) * (2.0 * math.pi / full_width)
    cosine, sine = np.cos(angle), np.sin(angle)
    upper = np.concatenate([cosine, -sine], axis=2)
    lower = np.concatenate([sine, cosine], axis=2)
    return np.concatenate([upper, lower], axis=1).astype(ml_dtypes.bfloat16)


def channel_weights(channel_flags):
    width = channel_flags.shape[0]
    angle = jnp.arange(width, dtype=F32) * (2.0 * math.pi / width)
    taper = (
        0.35875
        - 0.48829 * jnp.cos(angle)
        + 0.14128 * jnp.cos(2.0 * angle)
        - 0.01168 * jnp.cos(3.0 * angle)
    )
    return taper * channel_flags.astype(F32)


def taper_kernel(split, first_time, me_ref, order_ref, weight_ref, vis_ref, *refs):
    out_refs, energy_ref, wide_ref = refs[:-2], refs[-2], refs[-1]
    rows, parts, times, sub = vis_ref.shape
    count = times // 2
    me = me_ref[0]
    pick = (lax.broadcasted_iota(jnp.int32, (rows, rows), 1) == order_ref[...]).astype(BF16)
    total = jnp.zeros((rows, sub), F32)
    for part in range(parts):
        lanes = slice(part * sub, (part + 1) * sub)
        wide = vis_ref[:, part].astype(F32).reshape(rows * times, sub)
        for c in range(wide_ref.shape[0]):
            wide_ref[c] = wide[:, c * LANES : (c + 1) * LANES]
        for s in range(count):
            time = first_time + lax.rem(me + s, count)
            here = [wide_ref[c, pl.ds(time, rows, stride=times), :] for c in range(wide_ref.shape[0])]
            here = jnp.concatenate(here, axis=1).astype(BF16)
            moved = jnp.dot(pick, here, preferred_element_type=F32)
            tapered = (moved * weight_ref[...]).astype(BF16)
            if split:
                out_refs[s][:, lanes] = tapered
            else:
                blocks = out_refs[0].shape[0]
                out_refs[0][:, s, :, lanes] = tapered.reshape(blocks, rows // blocks, sub)
            square = tapered.astype(F32)
            total = total + square * square
    energy_ref[...] = lax.dot_general(
        jnp.ones((8, sub), F32),
        total,
        (((1,), (1,)), ((), ())),
        precision=HIGHEST,
        preferred_element_type=F32,
    )


def taper(split, first_time, blocks, me, order, weight, vis):
    rows, parts, times, sub = vis.shape
    count, lanes = times // 2, parts * sub
    if split:
        outs = [jax.ShapeDtypeStruct((rows, lanes), BF16)] * count
    else:
        outs = [jax.ShapeDtypeStruct((blocks, count, rows // blocks, lanes), BF16)]
    outs = outs + [jax.ShapeDtypeStruct((8, rows), F32)]
    return pl.pallas_call(
        functools.partial(taper_kernel, split, first_time),
        out_shape=outs,
        in_specs=[SMEM, VMEM, VMEM, VMEM],
        out_specs=[VMEM] * len(outs),
        scratch_shapes=[pltpu.VMEM((sub // LANES, rows * times, LANES), F32)],
        compiler_params=params(),
        cost_estimate=cost(2 * count * rows * rows * lanes, 4 * count * rows * lanes),
        name="taper_rows",
    )(me, order, weight, vis)


def delay_kernel(me_ref, matrix_ref, *refs):
    x_refs, out_refs, mixed = refs[:4], refs[4:8], refs[8]
    half = x_refs[0].shape[1] // 2
    me = me_ref[0]
    x = [ref[...].astype(F32) for ref in x_refs]
    a, b, c, d = x[0] + x[2], x[0] - x[2], x[1] + x[3], x[1] - x[3]
    turned = jnp.concatenate([-d[:, half:], d[:, :half]], axis=1)
    for r, value in enumerate((a + c, b + turned, a - c, b - turned)):
        if r:
            turns = lax.rem(r * me, 4)
            real = jnp.where(turns == 0, 1.0, jnp.where(turns == 2, -1.0, 0.0)).astype(F32)
            imag = jnp.where(turns == 3, 1.0, jnp.where(turns == 1, -1.0, 0.0)).astype(F32)
            if r == 2:
                value = value * real
            else:
                other = jnp.concatenate([-value[:, half:], value[:, :half]], axis=1)
                value = value * real + other * imag
        mixed[r] = value.astype(BF16)
    for s in range(4):
        r = lax.rem(me + s, 4)
        out_refs[s][...] = jnp.dot(mixed[r], matrix_ref[r], preferred_element_type=F32).astype(BF16)


def delay_transform(me, matrices, pieces):
    rows, lanes = pieces[0].shape
    block = min(rows, 256)
    tile = pl.BlockSpec((block, lanes), lambda i: (i, 0))
    return pl.pallas_call(
        delay_kernel,
        grid=(rows // block,),
        out_shape=[jax.ShapeDtypeStruct((rows, lanes), BF16)] * 4,
        in_specs=[SMEM, pl.BlockSpec(matrices.shape, lambda i: (0, 0, 0))] + [tile] * 4,
        out_specs=[tile] * 4,
        scratch_shapes=[pltpu.VMEM((4, block, lanes), BF16)],
        compiler_params=params(),
        cost_estimate=cost(8 * rows * lanes * lanes, 16 * rows * lanes + matrices.size * 2),
        name="delay_transform",
    )(me, matrices, *pieces)


def pair_weights_kernel(first_ref, second_ref, energy_ref, slot_ref, high_ref, low_ref, group_ref):
    rows = energy_ref.shape[1]
    pairs = first_ref.shape[1]
    place = lax.broadcasted_iota(jnp.int32, (rows, pairs), 0)
    contract_last = (((1,), (1,)), ((), ()))
    counts = lax.dot_general(
        (place == first_ref[...]).astype(BF16),
        (place == second_ref[...]).astype(BF16),
        contract_last,
        preferred_element_type=F32,
    )
    inverse = 1.0 / energy_ref[...]
    scale = inverse * jnp.sqrt(inverse)
    weighted = counts * scale
    high = weighted.astype(BF16)
    high_ref[...] = high
    low_ref[...] = (weighted - high.astype(F32)).astype(BF16)
    partner = lax.dot_general(
        jnp.broadcast_to(inverse, (8, rows)),
        counts,
        contract_last,
        precision=HIGHEST,
        preferred_element_type=F32,
    )[0:1]
    slots = group_ref.shape[0]
    member = lax.broadcasted_iota(jnp.int32, (slots, rows), 0) == slot_ref[...]
    denom = jnp.sum(jnp.where(member, inverse * partner, 0.0), axis=1, keepdims=True)
    group_ref[...] = jnp.where(member, scale, 0.0) / denom


def pair_weights(first, second, energy, slot, slots):
    rows = energy.shape[1]
    return pl.pallas_call(
        pair_weights_kernel,
        out_shape=[
            jax.ShapeDtypeStruct((rows, rows), BF16),
            jax.ShapeDtypeStruct((rows, rows), BF16),
            jax.ShapeDtypeStruct((slots, rows), F32),
        ],
        in_specs=[VMEM] * 4,
        out_specs=[VMEM] * 3,
        compiler_params=params(),
        cost_estimate=cost(2 * rows * rows * first.shape[1], 4 * rows * rows),
        name="pair_weights",
    )(first, second, energy, slot)


def pair_kernel(packed, count, high_ref, low_ref, group_ref, *refs):
    z_refs, out_ref = refs[:-1], refs[-1]
    block = high_ref.shape[0]
    rows = high_ref.shape[1]
    lanes = z_refs[0].shape[-1]
    step = pl.program_id(0)
    start = pl.multiple_of(step * block, block)
    total = jnp.zeros((block, lanes), F32)
    for t in range(count):
        if packed:
            per = rows // z_refs[0].shape[0]
            here = slice(t * per, (t + 1) * per)
            window = z_refs[0][:, here].reshape(rows, lanes)
            own = z_refs[0][pl.ds(step * (block // per), block // per), here].reshape(block, lanes)
        else:
            window = z_refs[t][...]
            own = z_refs[t][pl.ds(start, block), :]
        mixed = jnp.dot(high_ref[...], window, preferred_element_type=F32)
        mixed = mixed + jnp.dot(low_ref[...], window, preferred_element_type=F32)
        total = total + own.astype(F32) * mixed
    half = lanes // 2
    cross = total[:, :half] + total[:, half:]
    part = jnp.dot(group_ref[...], cross, precision=HIGHEST, preferred_element_type=F32)

    @pl.when(step == 0)
    def _():
        out_ref[...] = part

    @pl.when(step > 0)
    def _():
        out_ref[...] += part


def pair_sums(packed, count, high, low, group, pieces):
    rows = high.shape[1]
    slots = group.shape[0]
    lanes = pieces[0].shape[-1]
    block = min(rows, 256)
    whole = [pl.BlockSpec(p.shape, lambda i, n=p.ndim: (0,) * n) for p in pieces]
    return pl.pallas_call(
        functools.partial(pair_kernel, packed, count),
        grid=(rows // block,),
        out_shape=jax.ShapeDtypeStruct((slots, lanes // 2), F32),
        in_specs=[
            pl.BlockSpec((block, rows), lambda i: (i, 0)),
            pl.BlockSpec((block, rows), lambda i: (i, 0)),
            pl.BlockSpec((slots, block), lambda i: (0, i)),
        ]
        + whole,
        out_specs=pl.BlockSpec((slots, lanes // 2), lambda i: (0, 0)),
        compiler_params=params(),
        cost_estimate=cost(4 * count * rows * rows * lanes, 2 * count * rows * lanes),
        name="pair_sums",
    )(high, low, group, *pieces)


def interleave_kernel(me_ref, *refs):
    pieces, out_ref = refs[:-1], refs[-1]
    count = len(pieces)
    width = pieces[0].shape[1]
    me = me_ref[0]
    row = lax.broadcasted_iota(jnp.int32, (width, count * width), 0)
    column = lax.broadcasted_iota(jnp.int32, (width, count * width), 1)
    total = jnp.zeros(out_ref.shape, F32)
    for s in range(count):
        r = lax.rem(me + count - s, count)
        pick = (column == row * count + r).astype(F32)
        total = total + jnp.dot(pieces[s][...], pick, precision=HIGHEST, preferred_element_type=F32)
    out_ref[...] = total


def interleave(me, pieces):
    groups, width = pieces[0].shape
    return pl.pallas_call(
        interleave_kernel,
        out_shape=jax.ShapeDtypeStruct((groups, width * len(pieces)), F32),
        in_specs=[SMEM] + [VMEM] * len(pieces),
        out_specs=VMEM,
        compiler_params=params(),
        name="interleave_delays",
    )(me, *pieces)


def window_places(pair_list, owner, block_count, peer, band_count):
    owned = block_count * peer
    local = pair_list % owned
    source = jnp.where(pair_list < owned, owner, (owner + band_count - 1) % band_count)
    return (local // peer) * (band_count * peer) + source * peer + local % peer


def assemble_kernel(energy_ref, *refs):
    pieces, out_ref = refs[:-1], refs[-1]
    blocks, height, lanes = out_ref.shape
    per = pieces[0].shape[0] // blocks
    for t, piece in enumerate(pieces):
        out_ref[:, t * per : (t + 1) * per] = piece[...].reshape(blocks, per, lanes)
    extra = height - per * len(pieces)
    row = lax.broadcasted_iota(jnp.int32, (blocks, extra, lanes), 1)
    rest = jnp.broadcast_to(energy_ref[...], (blocks, extra, lanes))
    block = jnp.zeros((blocks, extra, lanes), F32)
    for k in range(ENERGY_PARTS):
        part = rest.astype(BF16).astype(F32)
        block = jnp.where(row == k, part, block)
        rest = rest - part
    out_ref[:, per * len(pieces) :] = block.astype(BF16)


def assemble(energy, blocks, pieces):
    rows, lanes = pieces[0].shape
    energy = energy.reshape(blocks, 1, rows // blocks)
    energy = jnp.pad(energy, ((0, 0), (0, 0), (0, lanes - rows // blocks)))
    height = len(pieces) * (rows // blocks) + EXTRA_ROWS
    return pl.pallas_call(
        assemble_kernel,
        out_shape=jax.ShapeDtypeStruct((blocks, height, lanes), BF16),
        in_specs=[VMEM] * (1 + len(pieces)),
        out_specs=VMEM,
        compiler_params=params(),
        cost_estimate=cost(rows * lanes, 4 * len(pieces) * rows * lanes),
        name="assemble",
    )(energy, *pieces)


def on_device(matrices, visibilities, send_order, channel_flags, group_ids, pair_list):
    band_count = lax.axis_size("band")
    block_count = lax.axis_size("bl")
    rows, times, parts, sub = visibilities.shape
    peer = rows // (band_count * block_count)
    column = band_count * peer
    lanes = parts * sub
    band = lax.axis_index("band").astype(jnp.int32)
    me = band.reshape(1)

    order = send_order[0].reshape(band_count, block_count, peer).transpose(1, 0, 2).reshape(rows, 1)
    weight = lax.dynamic_slice(channel_weights(channel_flags), (band * sub,), (sub,))
    weight = weight.reshape(1, sub)
    vis = visibilities.transpose(0, 2, 1, 3)

    *late, energy_late = taper(True, times // 2, block_count, me, order, weight, vis)
    late, vis = lax.optimization_barrier((late, vis))
    first_half, energy_first = taper(False, 0, block_count, me, order, weight, vis)

    energy = sum(spread([energy_first[0] + energy_late[0]] * band_count))

    tables = spread([jnp.concatenate([pair_list.reshape(-1), group_ids])] * band_count)
    owners = [(band + band_count - s) % band_count for s in range(band_count)]
    place = jnp.concatenate(
        [
            window_places(table[: pair_list.size].reshape(-1, 2), owner, block_count, peer, band_count)
            for table, owner in zip(tables, owners)
        ]
    ).T
    slot = jnp.zeros((block_count, band_count, peer), jnp.int32)
    for s, (table, owner) in enumerate(zip(tables, owners)):
        groups = table[pair_list.size :].reshape(block_count, 1, peer)
        groups = groups + GRP_DEV * ((band_count - s) % band_count)
        slot = jnp.where(jnp.arange(band_count)[None, :, None] == owner, groups, slot)

    early = lax.all_to_all(first_half, "bl", split_axis=0, concat_axis=0, tiled=True)
    late = spread(delay_transform(me, matrices, spread(late)))
    late = assemble(energy, block_count, late)
    late = lax.all_to_all(late, "bl", split_axis=0, concat_axis=0, tiled=True)

    early = [early[:, s].reshape(rows, lanes) for s in range(band_count)]
    early = spread(delay_transform(me, matrices, spread(early)))

    energy = late[:, band_count * column :][:, :ENERGY_PARTS, :column].astype(F32).sum(axis=1)
    energy = energy.reshape(1, rows) / (parts * times) + 1e-06
    high, low, group = pair_weights(
        place[0:1], place[1:2], energy, slot.reshape(1, rows), GRP_DEV * band_count
    )
    sums = pair_sums(True, band_count, high, low, group, [late])
    sums = sums + pair_sums(False, band_count, high, low, group, early)
    sums = sums.reshape(band_count, GRP_DEV, sub)
    return interleave(me, spread([sums[s] for s in range(band_count)]))


def solution(mesh):
    band_count = mesh.shape["band"]

    def whole(visibilities, send_order, channel_flags, group_ids, pair_list):
        full_width = visibilities.shape[3]
        matrices = jnp.asarray(class_matrices(full_width, band_count))
        mapped = jax.shard_map(
            on_device,
            mesh=mesh,
            in_specs=(
                P(),
                P("bl", None, None, "band"),
                P("bl", None),
                P(),
                P(("band", "bl")),
                P(("band", "bl"), None),
            ),
            out_specs=P(("band", "bl"), None),
            check_vma=False,
        )
        return mapped(matrices, visibilities, send_order, channel_flags, group_ids, pair_list)

    return whole
```

```python
import functools
import math

import jax
import jax.numpy as jnp
import ml_dtypes
import numpy as np
from jax import lax
from jax.experimental import pallas as pl
from jax.experimental.pallas import tpu as pltpu
from jax.sharding import PartitionSpec as P

GRP_DEV = 16
LANES = 128
DELAY_COST = 800
BF16_PARTS = 3
EXTRA_ROWS = 16
HIGHEST = lax.Precision.HIGHEST
VMEM_LIMIT = 28 * 1024 * 1024
F32 = jnp.float32
BF16 = jnp.bfloat16
VMEM = pl.BlockSpec(memory_space=pltpu.VMEM)
SMEM = pl.BlockSpec(memory_space=pltpu.SMEM)


def shifted(value, axis, steps):
    count = lax.axis_size(axis)
    pairs = [(source, (source + steps) % count) for source in range(count)]
    return lax.ppermute(value, axis, pairs)


def spread(pieces):
    return [pieces[0]] + [shifted(pieces[s], "band", s) for s in range(1, len(pieces))]


def cost(flops, bytes_accessed):
    return pl.CostEstimate(flops=flops, bytes_accessed=bytes_accessed, transcendentals=0)


def params(limit=VMEM_LIMIT):
    return pltpu.CompilerParams(vmem_limit_bytes=limit)


def class_matrices(full_width, classes):
    sub = full_width // classes
    channel = np.arange(sub)[None, :, None]
    delay = classes * np.arange(sub)[None, None, :] + np.arange(classes)[:, None, None]
    angle = (channel * delay % full_width) * (2.0 * math.pi / full_width)
    cosine, sine = np.cos(angle), np.sin(angle)
    upper = np.concatenate([cosine, -sine], axis=2)
    lower = np.concatenate([sine, cosine], axis=2)
    return np.concatenate([upper, lower], axis=1).astype(ml_dtypes.bfloat16)


def taper_window(full_width):
    angle = np.arange(full_width) * (2.0 * math.pi / full_width)
    window = (
        0.35875
        - 0.48829 * np.cos(angle)
        + 0.14128 * np.cos(2.0 * angle)
        - 0.01168 * np.cos(3.0 * angle)
    )
    return window.reshape(1, -1).astype(np.float32)


def tiles_of(ref, where, start, count, column):
    tiles = [ref[where, pl.ds((start + c) * column, column), :] for c in range(count)]
    return jnp.concatenate([t.reshape(-1, LANES) for t in tiles], axis=1)


def taper_kernel(times, parts, band_count, me_ref, order_ref, window_ref, flags_ref, vis_ref, *refs):
    early_ref, late_refs = refs[0], refs[1:-4]
    slab_ref, early_buf, late_buf, sems = refs[-4:]
    step = pl.program_id(0)
    slabs, rows, _ = slab_ref.shape
    height = vis_ref.shape[0] // slabs
    block = jnp.transpose(vis_ref[...].reshape(height, slabs, LANES), (1, 0, 2))
    slab_ref[:, pl.ds(pl.multiple_of(step * height, height), height), :] = block

    @pl.when(step == pl.num_programs(0) - 1)
    def _():
        blocks = early_buf.shape[0]
        count = len(late_refs)
        column = rows // blocks
        peer = column // band_count
        tiles = slabs // times
        sub = tiles // parts * LANES
        me = me_ref[0]
        here = pl.ds(pl.multiple_of(me * sub, sub), sub)
        weight = window_ref[:, here] * flags_ref[:, here].astype(F32)
        weight = jnp.concatenate([weight] * parts, axis=1)
        order = jnp.transpose(jnp.broadcast_to(order_ref[...].astype(F32), (LANES, rows)))
        if peer % 8 == 0:
            order = order.reshape(band_count, blocks, peer, LANES).transpose(1, 0, 2, 3)
            order = order.reshape(rows, LANES)
        lane = lax.broadcasted_iota(jnp.int32, (rows, LANES), 1)
        pick = [(lane + c == order.astype(jnp.int32)).astype(BF16) for c in range(0, rows, LANES)]
        pick = jnp.concatenate(pick, axis=1)
        total = jnp.zeros((rows, LANES), F32)
        copies = []
        for half in (1, 0):
            for s in range(count):
                time = half * count + lax.rem(me + s, count)
                source = [
                    slab_ref[(time * (tiles // parts) + tile) * parts + part]
                    for part in range(parts)
                    for tile in range(tiles // parts)
                ]
                moved = jnp.dot(pick, jnp.concatenate(source, axis=1), preferred_element_type=F32)
                tapered = (moved * weight).astype(BF16)
                for c in range(tiles):
                    tile = tapered[:, c * LANES : (c + 1) * LANES]
                    wide = tile.astype(F32)
                    total = total + wide * wide
                    tile = tile.reshape(blocks, column, LANES)
                    if half:
                        late_buf[s, :, c * column : (c + 1) * column] = tile
                    else:
                        start = (s * tiles + c) * column
                        early_buf[:, start : start + column] = tile
                if half:
                    copy = pltpu.make_async_copy(late_buf.at[s], late_refs[s], sems.at[s])
                else:
                    where = pl.ds(s * tiles * column, tiles * column)
                    copy = pltpu.make_async_copy(
                        early_buf.at[:, where], early_ref.at[:, where], sems.at[count + s]
                    )
                copy.start()
                copies.append(copy)
        energy = lax.dot_general(
            jnp.ones((EXTRA_ROWS, LANES), F32),
            total,
            (((1,), (1,)), ((), ())),
            precision=HIGHEST,
            preferred_element_type=F32,
        )
        row = lax.broadcasted_iota(jnp.int32, energy.shape, 0)
        rest, extra = energy, jnp.zeros_like(energy)
        for k in range(BF16_PARTS):
            part = rest.astype(BF16).astype(F32)
            extra = jnp.where(row == k, part, extra)
            rest = rest - part
        start = count * tiles * column
        for j in range(blocks):
            mine = extra[:, j * column : (j + 1) * column]
            mine = jnp.concatenate([mine, jnp.zeros((EXTRA_ROWS, LANES - column), F32)], axis=1)
            early_buf[j, start:] = mine.astype(BF16)
        where = pl.ds(start, EXTRA_ROWS)
        copy = pltpu.make_async_copy(
            early_buf.at[:, where], early_ref.at[:, where], sems.at[2 * count]
        )
        copy.start()
        for copy in copies + [copy]:
            copy.wait()


def taper(band_count, blocks, me, order, window, flags, visibilities):
    rows, times, parts, sub = visibilities.shape
    count, lanes, tiles, steps = times // 2, parts * sub, sub // LANES, 4
    column = rows // blocks
    vis = visibilities.reshape(rows, times, parts, tiles, LANES).transpose(0, 1, 3, 2, 4)
    vis = vis.reshape(rows * times * tiles * parts, LANES)
    piece = (blocks, parts * tiles * column, LANES)
    early = (blocks, count * parts * tiles * column + EXTRA_ROWS, LANES)
    return pl.pallas_call(
        functools.partial(taper_kernel, times, parts, band_count),
        grid=(steps,),
        out_shape=[jax.ShapeDtypeStruct(shape, BF16) for shape in [early] + [piece] * count],
        in_specs=[
            SMEM,
            pl.BlockSpec(order.shape, lambda i: (0, 0)),
            pl.BlockSpec(window.shape, lambda i: (0, 0)),
            pl.BlockSpec(flags.shape, lambda i: (0, 0)),
            pl.BlockSpec((vis.shape[0] // steps, LANES), lambda i: (i, 0)),
        ],
        out_specs=[pl.BlockSpec(memory_space=pl.ANY)] * (1 + count),
        scratch_shapes=[
            pltpu.VMEM((vis.shape[0] // rows, rows, LANES), BF16),
            pltpu.VMEM(early, BF16),
            pltpu.VMEM((count,) + piece, BF16),
            pltpu.SemaphoreType.DMA((2 * count + 1,)),
        ],
        compiler_params=params(60 * 1024 * 1024),
        cost_estimate=cost(2 * times * rows * rows * lanes, 4 * times * rows * lanes),
        name="taper_rows",
    )(me, order, window, flags, vis)


def delay_kernel(me_ref, matrix_ref, *refs):
    x_refs, out_refs, mixed = refs[:4], refs[4:8], refs[8]
    blocks, height, _ = x_refs[0].shape
    tiles = mixed.shape[2] // LANES
    column = height // tiles
    half = mixed.shape[2] // 2
    me = me_ref[0]
    x = [tiles_of(ref, slice(None), 0, tiles, column).astype(F32) for ref in x_refs]
    a, b, c, d = x[0] + x[2], x[0] - x[2], x[1] + x[3], x[1] - x[3]
    turned = jnp.concatenate([-d[:, half:], d[:, :half]], axis=1)
    for r, value in enumerate((a + c, b + turned, a - c, b - turned)):
        if r:
            turns = lax.rem(r * me, 4)
            real = jnp.where(turns == 0, 1.0, jnp.where(turns == 2, -1.0, 0.0)).astype(F32)
            imag = jnp.where(turns == 3, 1.0, jnp.where(turns == 1, -1.0, 0.0)).astype(F32)
            if r == 2:
                value = value * real
            else:
                other = jnp.concatenate([-value[:, half:], value[:, :half]], axis=1)
                value = value * real + other * imag
        mixed[r] = value.astype(BF16)
    for s in range(4):
        r = lax.rem(me + s, 4)
        out = jnp.dot(mixed[r], matrix_ref[r], preferred_element_type=F32).astype(BF16)
        for c in range(tiles):
            tile = out[:, c * LANES : (c + 1) * LANES].reshape(blocks, column, LANES)
            out_refs[s][:, c * column : (c + 1) * column] = tile


def delay_transform(me, matrices, pieces):
    _, lanes, _ = matrices.shape
    blocks, height, _ = pieces[-1].shape
    column = height // (lanes // LANES)
    group = max(1, 256 // column)
    tile = pl.BlockSpec((group, height, LANES), lambda i: (i, 0, 0))
    return pl.pallas_call(
        delay_kernel,
        grid=(blocks // group,),
        out_shape=[jax.ShapeDtypeStruct((blocks, height, LANES), BF16)] * 4,
        in_specs=[SMEM, pl.BlockSpec(matrices.shape, lambda i: (0, 0, 0))] + [tile] * 4,
        out_specs=[tile] * 4,
        scratch_shapes=[pltpu.VMEM((4, group * column, lanes), BF16)],
        compiler_params=params(),
        cost_estimate=cost(DELAY_COST * blocks * column * lanes * lanes, 16 * blocks * height * LANES),
        name="delay_transform",
    )(me, matrices, *pieces)


def pair_weights_kernel(first_ref, second_ref, energy_ref, slot_ref, mix_ref, group_ref):
    rows = energy_ref.shape[1]
    pairs = first_ref.shape[1]
    place = lax.broadcasted_iota(jnp.int32, (rows, pairs), 0)
    contract_last = (((1,), (1,)), ((), ()))
    counts = lax.dot_general(
        (place == first_ref[...]).astype(BF16),
        (place == second_ref[...]).astype(BF16),
        contract_last,
        preferred_element_type=F32,
    )
    inverse = 1.0 / energy_ref[...]
    scale = inverse * jnp.sqrt(inverse)
    weighted = counts * scale
    mix_ref[...] = weighted.astype(BF16)
    partner = lax.dot_general(
        jnp.broadcast_to(inverse, (8, rows)),
        counts,
        contract_last,
        precision=HIGHEST,
        preferred_element_type=F32,
    )[0:1]
    slots = group_ref.shape[0]
    member = lax.broadcasted_iota(jnp.int32, (slots, rows), 0) == slot_ref[...]
    denom = jnp.sum(jnp.where(member, inverse * partner, 0.0), axis=1, keepdims=True)
    group_ref[...] = jnp.where(member, scale, 0.0) / denom


def pair_weights(first, second, energy, slot, slots):
    rows = energy.shape[1]
    return pl.pallas_call(
        pair_weights_kernel,
        out_shape=[
            jax.ShapeDtypeStruct((rows, rows), BF16),
            jax.ShapeDtypeStruct((slots, rows), F32),
        ],
        in_specs=[VMEM] * 4,
        out_specs=[VMEM] * 2,
        compiler_params=params(),
        cost_estimate=cost(2 * rows * rows * first.shape[1], 4 * rows * rows),
        name="pair_weights",
    )(first, second, energy, slot)


def pair_kernel(count, mix_ref, group_ref, *refs):
    z_refs, out_ref = refs[:-1], refs[-1]
    block, rows = mix_ref.shape
    column = rows // z_refs[0].shape[0]
    lanes = 2 * out_ref.shape[1]
    tiles = lanes // LANES
    step = pl.program_id(0)
    mine = pl.ds(step * (block // column), block // column)
    total = jnp.zeros((block, lanes), F32)
    for t in range(count):
        ref, start = (z_refs[0], t * tiles) if len(z_refs) == 1 else (z_refs[t], 0)
        window = tiles_of(ref, slice(None), start, tiles, column)
        own = tiles_of(ref, mine, start, tiles, column)
        mixed = jnp.dot(mix_ref[...], window, preferred_element_type=F32)
        total = total + own.astype(F32) * mixed
    half = lanes // 2
    cross = total[:, :half] + total[:, half:]
    part = jnp.dot(group_ref[...], cross, precision=HIGHEST, preferred_element_type=F32)

    @pl.when(step == 0)
    def _():
        out_ref[...] = part

    @pl.when(step > 0)
    def _():
        out_ref[...] += part


def pair_sums(count, half, mix, group, pieces):
    rows = mix.shape[1]
    slots = group.shape[0]
    block = min(rows, 256)
    whole = [pl.BlockSpec(p.shape, lambda i: (0, 0, 0)) for p in pieces]
    return pl.pallas_call(
        functools.partial(pair_kernel, count),
        grid=(rows // block,),
        out_shape=jax.ShapeDtypeStruct((slots, half), F32),
        in_specs=[
            pl.BlockSpec((block, rows), lambda i: (i, 0)),
            pl.BlockSpec((slots, block), lambda i: (0, i)),
        ]
        + whole,
        out_specs=pl.BlockSpec((slots, half), lambda i: (0, 0)),
        compiler_params=params(),
        cost_estimate=cost(4 * count * rows * rows * half, 4 * count * rows * half),
        name="pair_sums",
    )(mix, group, *pieces)


def interleave_kernel(me_ref, *refs):
    pieces, out_ref = refs[:-1], refs[-1]
    count = len(pieces)
    width = pieces[0].shape[1]
    me = me_ref[0]
    row = lax.broadcasted_iota(jnp.int32, (width, count * width), 0)
    column = lax.broadcasted_iota(jnp.int32, (width, count * width), 1)
    total = 0.0
    for s in range(count):
        r = lax.rem(me + count - s, count)
        pick = (column == row * count + r).astype(BF16)
        rest, parts = pieces[s][...], []
        for _ in range(BF16_PARTS):
            parts.append(rest.astype(BF16))
            rest = rest - parts[-1].astype(F32)
        parts = jnp.concatenate(parts, axis=0)
        total = total + jnp.dot(parts, pick, preferred_element_type=F32)
    groups = out_ref.shape[0]
    out_ref[...] = sum(total[k * groups : (k + 1) * groups] for k in range(BF16_PARTS))


def interleave(me, pieces):
    groups, width = pieces[0].shape
    return pl.pallas_call(
        interleave_kernel,
        out_shape=jax.ShapeDtypeStruct((groups, width * len(pieces)), F32),
        in_specs=[SMEM] + [VMEM] * len(pieces),
        out_specs=VMEM,
        compiler_params=params(),
        name="interleave_delays",
    )(me, *pieces)


def window_places(pair_list, owner, block_count, peer, band_count):
    owned = block_count * peer
    local = pair_list % owned
    source = jnp.where(pair_list < owned, owner, (owner + band_count - 1) % band_count)
    return (local // peer) * (band_count * peer) + source * peer + local % peer


def on_device(matrices, window, visibilities, send_order, channel_flags, group_ids, pair_list):
    band_count = lax.axis_size("band")
    block_count = lax.axis_size("bl")
    rows, times, parts, sub = visibilities.shape
    peer = rows // (band_count * block_count)
    column = band_count * peer
    height = parts * sub // LANES * column
    band = lax.axis_index("band").astype(jnp.int32)
    me = band.reshape(1)

    order = send_order
    if peer % 8:
        order = order.reshape(band_count, block_count, peer).transpose(1, 0, 2).reshape(1, rows)
    flags = channel_flags.reshape(1, -1)
    early, *late = taper(band_count, block_count, me, order, window, flags, visibilities)

    early = lax.all_to_all(early, "bl", split_axis=0, concat_axis=0, tiled=True)
    late = spread(delay_transform(me, matrices, spread(late)))
    late = jnp.concatenate(late, axis=1)
    late = lax.all_to_all(late, "bl", split_axis=0, concat_axis=0, tiled=True)

    energy = early[:, band_count * height :][:, :BF16_PARTS, :column].astype(F32).sum(axis=1)
    early = [early] + [early[:, s * height : (s + 1) * height] for s in range(1, band_count)]
    early = delay_transform(me, matrices, spread(early))

    small = jnp.concatenate(
        [energy.reshape(-1), pair_list.reshape(-1).astype(F32), group_ids.astype(F32)]
    )
    early, small = lax.optimization_barrier((early, small))
    early = spread(early)
    small = spread([small] * band_count)
    energy = sum(table[:rows] for table in small).reshape(1, rows) / (parts * times) + 1e-06
    tables = [table[rows:].astype(jnp.int32) for table in small]
    owners = [(band + band_count - s) % band_count for s in range(band_count)]
    place = jnp.concatenate(
        [
            window_places(table[: pair_list.size].reshape(-1, 2), owner, block_count, peer, band_count)
            for table, owner in zip(tables, owners)
        ]
    ).T
    slot = jnp.zeros((block_count, band_count, peer), jnp.int32)
    for s, (table, owner) in enumerate(zip(tables, owners)):
        groups = table[pair_list.size :].reshape(block_count, 1, peer)
        groups = groups + GRP_DEV * ((band_count - s) % band_count)
        slot = jnp.where(jnp.arange(band_count)[None, :, None] == owner, groups, slot)
    mix, group = pair_weights(
        place[0:1], place[1:2], energy, slot.reshape(1, rows), GRP_DEV * band_count
    )
    sums = pair_sums(band_count, sub, mix, group, early)
    sums = sums + pair_sums(band_count, sub, mix, group, [late])
    sums = sums.reshape(band_count, GRP_DEV, sub)
    return interleave(me, spread([sums[s] for s in range(band_count)]))


def solution(mesh):
    band_count = mesh.shape["band"]

    def whole(visibilities, send_order, channel_flags, group_ids, pair_list):
        full_width = visibilities.shape[3]
        matrices = jnp.asarray(class_matrices(full_width, band_count))
        window = jnp.asarray(taper_window(full_width))
        mapped = jax.shard_map(
            on_device,
            mesh=mesh,
            in_specs=(
                P(),
                P(),
                P("bl", None, None, "band"),
                P("bl", None),
                P(),
                P(("band", "bl")),
                P(("band", "bl"), None),
            ),
            out_specs=P(("band", "bl"), None),
            check_vma=False,
        )
        return mapped(
            matrices, window, visibilities, send_order, channel_flags, group_ids, pair_list
        )

    return whole
```

```python
import functools
import math

import jax
import jax.numpy as jnp
import ml_dtypes
import numpy as np
from jax import lax
from jax.experimental import pallas as pl
from jax.experimental.pallas import tpu as pltpu
from jax.sharding import PartitionSpec as P

GRP_DEV = 16
LANES = 128
LATE_COST = 10**9
EARLY_COST = 10**9
HALVES = 2
LOADS = 8
PAIR_ROWS = 2
BF16_PARTS = 3
EXTRA_ROWS = 16
HIGHEST = lax.Precision.HIGHEST
VMEM_LIMIT = 20 * 1024 * 1024
F32 = jnp.float32
BF16 = jnp.bfloat16
VMEM = pl.BlockSpec(memory_space=pltpu.VMEM)
SMEM = pl.BlockSpec(memory_space=pltpu.SMEM)
HBM = pl.BlockSpec(memory_space=pltpu.HBM)


def shifted(value, axis, steps):
    count = lax.axis_size(axis)
    pairs = [(source, (source + steps) % count) for source in range(count)]
    return lax.ppermute(value, axis, pairs)


def spread(pieces):
    return [pieces[0]] + [shifted(pieces[s], "band", s) for s in range(1, len(pieces))]


def cost(flops, bytes_accessed):
    return pl.CostEstimate(flops=flops, bytes_accessed=bytes_accessed, transcendentals=0)


def params(limit=VMEM_LIMIT):
    return pltpu.CompilerParams(vmem_limit_bytes=limit)


def class_matrices(full_width, classes):
    sub = full_width // classes
    channel = np.arange(sub)[None, :, None]
    delay = classes * np.arange(sub)[None, None, :] + np.arange(classes)[:, None, None]
    angle = (channel * delay % full_width) * (2.0 * math.pi / full_width)
    cosine, sine = np.cos(angle), np.sin(angle)
    upper = np.concatenate([cosine, -sine], axis=2)
    lower = np.concatenate([sine, cosine], axis=2)
    return np.concatenate([upper, lower], axis=1).astype(ml_dtypes.bfloat16)


def taper_window(full_width):
    angle = np.arange(full_width) * (2.0 * math.pi / full_width)
    window = (
        0.35875
        - 0.48829 * np.cos(angle)
        + 0.14128 * np.cos(2.0 * angle)
        - 0.01168 * np.cos(3.0 * angle)
    )
    return window.reshape(1, -1).astype(np.float32)


def tiles_of(ref, where, start, count, column):
    tiles = [ref[where, pl.ds((start + c) * column, column), :] for c in range(count)]
    return jnp.concatenate([t.reshape(-1, LANES) for t in tiles], axis=1)


def taper_kernel(times, parts, band_count, me_ref, order_ref, window_ref, flags_ref, vis_ref, *refs):
    early_ref, late_refs = refs[0], refs[1:-6]
    vis_buf, slab_ref, early_buf, late_buf, load_sems, sems = refs[-6:]
    slabs, rows, _ = slab_ref.shape
    chunks = load_sems.shape[0]
    height = rows // chunks
    loads = []
    for k in range(chunks):
        where = pl.ds(k * height * slabs, height * slabs)
        loads.append(
            pltpu.make_async_copy(vis_ref.at[where, :], vis_buf.at[where, :], load_sems.at[k])
        )
        loads[-1].start()
    blocks = early_buf.shape[0]
    count, halves = late_buf.shape[:2]
    column = rows // blocks
    peer = column // band_count
    tiles = slabs // times
    sub = tiles // parts * LANES
    me = me_ref[0]
    here = pl.ds(pl.multiple_of(me * sub, sub), sub)
    weight = window_ref[:, here] * flags_ref[:, here].astype(F32)
    weight = jnp.concatenate([weight] * parts, axis=1)
    order = jnp.transpose(jnp.broadcast_to(order_ref[...].astype(F32), (LANES, rows)))
    if peer % 8 == 0:
        order = order.reshape(band_count, blocks, peer, LANES).transpose(1, 0, 2, 3)
        order = order.reshape(rows, LANES)
    lane = lax.broadcasted_iota(jnp.int32, (rows, LANES), 1)
    pick = [(lane + c == order.astype(jnp.int32)).astype(BF16) for c in range(0, rows, LANES)]
    pick = jnp.concatenate(pick, axis=1)
    for k, load in enumerate(loads):
        load.wait()
        block = vis_buf[k * height * slabs : (k + 1) * height * slabs, :]
        block = jnp.transpose(block.reshape(height, slabs, LANES), (1, 0, 2))
        slab_ref[:, k * height : (k + 1) * height, :] = block
    total = jnp.zeros((rows, LANES), F32)
    copies = []
    for half in (1, 0):
        for s in range(count):
            time = half * count + lax.rem(me + s, count)
            source = [
                slab_ref[(time * (tiles // parts) + tile) * parts + part]
                for part in range(parts)
                for tile in range(tiles // parts)
            ]
            moved = jnp.dot(pick, jnp.concatenate(source, axis=1), preferred_element_type=F32)
            tapered = (moved * weight).astype(BF16)
            for c in range(tiles):
                tile = tapered[:, c * LANES : (c + 1) * LANES]
                wide = tile.astype(F32)
                total = total + wide * wide
                tile = tile.reshape(blocks, column, LANES)
                if half:
                    tile = tile.reshape(halves, blocks // halves, column, LANES)
                    late_buf[s, :, :, c * column : (c + 1) * column] = tile
                else:
                    start = (s * tiles + c) * column
                    early_buf[:, start : start + column] = tile
            if half:
                new = [
                    pltpu.make_async_copy(
                        late_buf.at[s, h], late_refs[h * count + s], sems.at[h * count + s]
                    )
                    for h in range(halves)
                ]
            else:
                where = pl.ds(s * tiles * column, tiles * column)
                new = [
                    pltpu.make_async_copy(
                        early_buf.at[:, where], early_ref.at[:, where], sems.at[halves * count + s]
                    )
                ]
            for copy in new:
                copy.start()
            copies += new
    energy = lax.dot_general(
        jnp.ones((EXTRA_ROWS, LANES), F32),
        total,
        (((1,), (1,)), ((), ())),
        precision=HIGHEST,
        preferred_element_type=F32,
    )
    row = lax.broadcasted_iota(jnp.int32, energy.shape, 0)
    rest, extra = energy, jnp.zeros_like(energy)
    for k in range(BF16_PARTS):
        part = rest.astype(BF16).astype(F32)
        extra = jnp.where(row == k, part, extra)
        rest = rest - part
    start = count * tiles * column
    for j in range(blocks):
        mine = extra[:, j * column : (j + 1) * column]
        mine = jnp.concatenate([mine, jnp.zeros((EXTRA_ROWS, LANES - column), F32)], axis=1)
        early_buf[j, start:] = mine.astype(BF16)
    where = pl.ds(start, EXTRA_ROWS)
    copy = pltpu.make_async_copy(
        early_buf.at[:, where], early_ref.at[:, where], sems.at[(halves + 1) * count]
    )
    copy.start()
    for copy in copies + [copy]:
        copy.wait()


def taper(band_count, blocks, me, order, window, flags, visibilities):
    rows, times, parts, sub = visibilities.shape
    count, lanes, tiles = times // 2, parts * sub, sub // LANES
    column = rows // blocks
    vis = visibilities.reshape(rows, times, parts, tiles, LANES).transpose(0, 1, 3, 2, 4)
    vis = vis.reshape(rows * times * tiles * parts, LANES)
    piece = (blocks // HALVES, parts * tiles * column, LANES)
    early = (blocks, count * parts * tiles * column + EXTRA_ROWS, LANES)
    return pl.pallas_call(
        functools.partial(taper_kernel, times, parts, band_count),
        out_shape=[jax.ShapeDtypeStruct(shape, BF16) for shape in [early] + [piece] * (HALVES * count)],
        in_specs=[SMEM, VMEM, VMEM, VMEM, HBM],
        out_specs=[HBM] * (1 + HALVES * count),
        scratch_shapes=[
            pltpu.VMEM(vis.shape, BF16),
            pltpu.VMEM((vis.shape[0] // rows, rows, LANES), BF16),
            pltpu.VMEM(early, BF16),
            pltpu.VMEM((count, HALVES) + piece, BF16),
            pltpu.SemaphoreType.DMA((LOADS,)),
            pltpu.SemaphoreType.DMA(((HALVES + 1) * count + 1,)),
        ],
        compiler_params=params(60 * 1024 * 1024),
        cost_estimate=cost(2 * times * rows * rows * lanes, 4 * times * rows * lanes),
        name="taper_rows",
    )(me, order, window, flags, vis)


def delay_kernel(half, me_ref, matrix_hbm, *refs):
    sources, outs = refs[:4], refs[4:8]
    x_refs, matrix_ref, mixed, out_buf, sems = refs[8:]
    blocks, height, _ = x_refs.shape[1:]
    lanes = mixed.shape[2]
    tiles = lanes // LANES
    column = height // tiles
    middle = lanes // 2
    me = me_ref[0]
    own = sources[0].at[pl.ds(half * blocks, blocks), pl.ds(0, height)]
    loads = [
        pltpu.make_async_copy(source, x_refs.at[s], sems.at[s])
        for s, source in enumerate([own] + [x.at[:, pl.ds(0, height)] for x in sources[1:]])
    ]
    loads.append(pltpu.make_async_copy(matrix_hbm, matrix_ref, sems.at[4]))
    for load in loads:
        load.start()
    for load in loads[:4]:
        load.wait()
    x = [tiles_of(x_refs.at[s], slice(None), 0, tiles, column).astype(F32) for s in range(4)]
    a, b, c, d = x[0] + x[2], x[0] - x[2], x[1] + x[3], x[1] - x[3]
    turned = jnp.concatenate([-d[:, middle:], d[:, :middle]], axis=1)
    for r, value in enumerate((a + c, b + turned, a - c, b - turned)):
        if r:
            turns = lax.rem(r * me, 4)
            real = jnp.where(turns == 0, 1.0, jnp.where(turns == 2, -1.0, 0.0)).astype(F32)
            imag = jnp.where(turns == 3, 1.0, jnp.where(turns == 1, -1.0, 0.0)).astype(F32)
            if r == 2:
                value = value * real
            else:
                other = jnp.concatenate([-value[:, middle:], value[:, :middle]], axis=1)
                value = value * real + other * imag
        mixed[r] = value.astype(BF16)
    loads[4].wait()
    stores = []
    for s in (1, 2, 3, 0):
        r = lax.rem(me + s, 4)
        out = jnp.dot(mixed[r], matrix_ref[r], preferred_element_type=F32).astype(BF16)
        for c in range(tiles):
            tile = out[:, c * LANES : (c + 1) * LANES].reshape(blocks, column, LANES)
            out_buf[s, :, c * column : (c + 1) * column] = tile
        stores.append(pltpu.make_async_copy(out_buf.at[s], outs[s], sems.at[5 + s]))
        stores[-1].start()
    for store in stores:
        store.wait()


def delay_transform(me, matrices, height, pieces, flops, half=0):
    _, lanes, _ = matrices.shape
    blocks = pieces[1].shape[0]
    piece = (blocks, height, LANES)
    rows = blocks * height * LANES // lanes
    return pl.pallas_call(
        functools.partial(delay_kernel, half),
        out_shape=[jax.ShapeDtypeStruct(piece, BF16)] * 4,
        in_specs=[SMEM] + [HBM] * 5,
        out_specs=[HBM] * 4,
        scratch_shapes=[
            pltpu.VMEM((4,) + piece, BF16),
            pltpu.VMEM(matrices.shape, BF16),
            pltpu.VMEM((4, rows, lanes), BF16),
            pltpu.VMEM((4,) + piece, BF16),
            pltpu.SemaphoreType.DMA((9,)),
        ],
        compiler_params=params(),
        cost_estimate=cost(flops, 16 * rows * lanes),
        name="delay_transform",
    )(me, matrices, *pieces)


def join_kernel(*refs):
    pieces, out_ref, buf, load_sems, store_sems = refs[:-4], *refs[-4:]
    count = len(pieces) // HALVES
    blocks, height, _ = pieces[0].shape
    loads, stores = [], []
    for k, piece in enumerate(pieces):
        loads.append(pltpu.make_async_copy(piece, buf.at[k], load_sems.at[k]))
        loads[-1].start()
    for k, load in enumerate(loads):
        load.wait()
        half, s = k // count, k % count
        where = out_ref.at[pl.ds(half * blocks, blocks), pl.ds(s * height, height)]
        stores.append(pltpu.make_async_copy(buf.at[k], where, store_sems.at[k]))
        stores[-1].start()
    for store in stores:
        store.wait()


def join(pieces):
    blocks, height, _ = pieces[0].shape
    out = (blocks * HALVES, height * (len(pieces) // HALVES), LANES)
    return pl.pallas_call(
        join_kernel,
        out_shape=jax.ShapeDtypeStruct(out, BF16),
        in_specs=[HBM] * len(pieces),
        out_specs=HBM,
        scratch_shapes=[
            pltpu.VMEM((len(pieces), blocks, height, LANES), BF16),
            pltpu.SemaphoreType.DMA((len(pieces),)),
            pltpu.SemaphoreType.DMA((len(pieces),)),
        ],
        compiler_params=params(),
        name="join_pieces",
    )(*pieces)


def pair_weights_kernel(peer, samples, height, me_ref, *refs):
    sources, mix_ref, group_ref, table_ref, sems = refs[:-4], *refs[-4:]
    band_count = len(sources)
    rows = mix_ref.shape[0]
    column = band_count * peer
    owned = rows // band_count
    me = me_ref[0]
    own = [sources[0]] + [x.at[:, pl.ds(height, EXTRA_ROWS)] for x in sources[1:]]
    loads = [pltpu.make_async_copy(x, table_ref.at[s], sems.at[s]) for s, x in enumerate(own)]
    for load in loads:
        load.start()
    for load in loads:
        load.wait()

    def line(table, start, count):
        return jnp.concatenate([table[start + k : start + k + 1] for k in range(count)], axis=1)

    energy, first, second, slot = 0.0, [], [], 0.0
    local = lax.broadcasted_iota(jnp.int32, (owned, rows), 0)
    place = lax.broadcasted_iota(jnp.int32, (owned, rows), 1)
    for s in range(band_count):
        owner = lax.rem(me + band_count - s, band_count)
        table = table_ref[s].astype(F32).reshape(-1, LANES)
        at = 0
        for _ in range(BF16_PARTS):
            energy = energy + line(table, at, rows // LANES)
            at += rows // LANES
        for out in (first, second):
            pair = line(table, at, PAIR_ROWS).astype(jnp.int32)
            at += PAIR_ROWS
            own = pair < owned
            pair = jnp.where(own, pair, pair - owned)
            source = jnp.where(own, owner, lax.rem(owner + band_count - 1, band_count))
            out.append(pair // peer * column + source * peer + pair % peer)
        groups = line(table, at, owned // LANES) + GRP_DEV * ((band_count - s) % band_count)
        here = local // peer * column + owner * peer + local % peer == place
        groups = jnp.broadcast_to(groups, (8, owned)).astype(BF16)
        slot = slot + jnp.dot(groups, here.astype(BF16), preferred_element_type=F32)
    energy = energy / samples + 1e-06
    place = lax.broadcasted_iota(jnp.int32, (rows, band_count * PAIR_ROWS * LANES), 0)
    contract_last = (((1,), (1,)), ((), ()))
    counts = lax.dot_general(
        (place == jnp.concatenate(first, axis=1)).astype(BF16),
        (place == jnp.concatenate(second, axis=1)).astype(BF16),
        contract_last,
        preferred_element_type=F32,
    )
    inverse = 1.0 / energy
    scale = inverse * jnp.sqrt(inverse)
    mix_ref[...] = (counts * scale).astype(BF16)
    partner = lax.dot_general(
        jnp.broadcast_to(inverse, (8, rows)),
        counts,
        contract_last,
        precision=HIGHEST,
        preferred_element_type=F32,
    )[0:1]
    slots = group_ref.shape[0]
    member = lax.broadcasted_iota(jnp.int32, (slots, rows), 0) == slot[0:1].astype(jnp.int32)
    denom = jnp.sum(jnp.where(member, inverse * partner, 0.0), axis=1, keepdims=True)
    group_ref[...] = jnp.where(member, scale, 0.0) / denom


def pair_weights(me, peer, samples, rows, height, tables):
    slots = GRP_DEV * len(tables)
    return pl.pallas_call(
        functools.partial(pair_weights_kernel, peer, samples, height),
        out_shape=[
            jax.ShapeDtypeStruct((rows, rows), BF16),
            jax.ShapeDtypeStruct((slots, rows), F32),
        ],
        in_specs=[SMEM] + [HBM] * len(tables),
        out_specs=[VMEM] * 2,
        scratch_shapes=[
            pltpu.VMEM((len(tables),) + tables[0].shape, BF16),
            pltpu.SemaphoreType.DMA((len(tables),)),
        ],
        compiler_params=params(),
        cost_estimate=cost(4 * rows * rows * rows, 4 * rows * rows),
        name="pair_weights",
    )(me, *tables)


def pair_kernel(by_hand, mix_ref, group_ref, before_ref, *refs):
    if by_hand:
        z_refs, out_ref, buf, sems = refs[:1], *refs[1:]
        height = buf.shape[2]
        loads = [
            pltpu.make_async_copy(z_refs[0].at[:, pl.ds(t * height, height)], buf.at[t], sems.at[t])
            for t in range(buf.shape[0])
        ]
        for load in loads:
            load.start()
        parts, count = 1, len(loads)
    else:
        z_refs, out_ref = refs[:-1], refs[-1]
        parts, count = HALVES, len(z_refs) // HALVES
    rows = mix_ref.shape[0]
    slots, half = out_ref.shape
    tiles = 2 * half // LANES
    column = rows // (parts * z_refs[0].shape[0])
    value = 0.0
    for t in range(count):
        if by_hand:
            loads[t].wait()
            window = tiles_of(buf.at[t], slice(None), 0, tiles, column)
        else:
            here = z_refs[t * parts : (t + 1) * parts]
            window = [tiles_of(ref, slice(None), 0, tiles, column) for ref in here]
            window = jnp.concatenate(window, axis=0)
        mixed = jnp.dot(mix_ref[...], window, preferred_element_type=F32)
        mixed = window.astype(F32) * mixed
        value = value + (mixed[:, :half] + mixed[:, half:])
    group = group_ref[...]
    group_high, value_high = group.astype(BF16), value.astype(BF16)
    group_low = (group - group_high.astype(F32)).astype(BF16)
    value_low = (value - value_high.astype(F32)).astype(BF16)
    both = jnp.concatenate([group_high, group_low], axis=0)
    part = jnp.dot(both, value_high, preferred_element_type=F32)
    part = part[:slots] + part[slots:]
    part = part + jnp.dot(group_high, value_low, preferred_element_type=F32)
    out_ref[...] = before_ref[...] + part


def pair_sums(mix, group, before, pieces):
    rows = mix.shape[1]
    half = before.shape[1]
    blocks, length, _ = pieces[0].shape
    by_hand = len(pieces) == 1
    scratch = []
    if by_hand:
        height = 2 * half // LANES * rows // blocks
        count = length // height
        scratch = [
            pltpu.VMEM((count, blocks, height, LANES), BF16),
            pltpu.SemaphoreType.DMA((count,)),
        ]
    else:
        count = len(pieces) // HALVES
    return pl.pallas_call(
        functools.partial(pair_kernel, by_hand),
        out_shape=jax.ShapeDtypeStruct(before.shape, F32),
        in_specs=[VMEM] * 3 + [HBM if by_hand else VMEM] * len(pieces),
        out_specs=VMEM,
        scratch_shapes=scratch,
        compiler_params=params(),
        cost_estimate=cost(4 * count * rows * rows * half, 4 * count * rows * half),
        name="pair_sums",
    )(mix, group, before, *pieces)


def interleave_kernel(me_ref, *refs):
    pieces, out_ref = refs[:-1], refs[-1]
    count = len(pieces)
    width = pieces[0].shape[1]
    me = me_ref[0]
    row = lax.broadcasted_iota(jnp.int32, (width, count * width), 0)
    column = lax.broadcasted_iota(jnp.int32, (width, count * width), 1)
    total = 0.0
    for s in range(count):
        r = lax.rem(me + count - s, count)
        pick = (column == row * count + r).astype(BF16)
        rest, parts = pieces[s][...], []
        for _ in range(BF16_PARTS):
            parts.append(rest.astype(BF16))
            rest = rest - parts[-1].astype(F32)
        parts = jnp.concatenate(parts, axis=0)
        total = total + jnp.dot(parts, pick, preferred_element_type=F32)
    groups = out_ref.shape[0]
    out_ref[...] = sum(total[k * groups : (k + 1) * groups] for k in range(BF16_PARTS))


def interleave(me, pieces):
    groups, width = pieces[0].shape
    return pl.pallas_call(
        interleave_kernel,
        out_shape=jax.ShapeDtypeStruct((groups, width * len(pieces)), F32),
        in_specs=[SMEM] + [VMEM] * len(pieces),
        out_specs=VMEM,
        compiler_params=params(),
        name="interleave_delays",
    )(me, *pieces)


def on_device(matrices, window, visibilities, send_order, channel_flags, group_ids, pair_list):
    band_count = lax.axis_size("band")
    block_count = lax.axis_size("bl")
    rows, times, parts, sub = visibilities.shape
    peer = rows // (band_count * block_count)
    column = band_count * peer
    height = parts * sub // LANES * column
    band = lax.axis_index("band").astype(jnp.int32)
    me = band.reshape(1)

    order = send_order
    if peer % 8:
        order = order.reshape(band_count, block_count, peer).transpose(1, 0, 2).reshape(1, rows)
    flags = channel_flags.reshape(1, -1)
    tables = jnp.concatenate([pair_list[:, 0], pair_list[:, 1], group_ids])
    tables = tables.astype(BF16).reshape(-1, LANES)
    early, *late = taper(band_count, block_count, me, order, window, flags, visibilities)

    early = lax.all_to_all(early, "bl", split_axis=0, concat_axis=0, tiled=True)
    late = [late[h * band_count : (h + 1) * band_count] for h in range(HALVES)]
    late = [spread(pieces) for pieces in late]
    late = [spread(delay_transform(me, matrices, height, pieces, LATE_COST)) for pieces in late]
    late = join([piece for pieces in late for piece in pieces])
    early, late = lax.optimization_barrier((early, late))
    late = lax.all_to_all(late, "bl", split_axis=0, concat_axis=0, tiled=True)

    some = block_count // HALVES
    energy = early[:, band_count * height :][:, :BF16_PARTS, :column]
    energy = energy.transpose(1, 0, 2).reshape(-1, LANES)
    table = jnp.concatenate([energy, tables], axis=0)
    table = jnp.pad(table, ((0, some * EXTRA_ROWS - table.shape[0]), (0, 0)))
    table = table.reshape(some, EXTRA_ROWS, LANES)
    pieces = [
        [
            early[h * some : (h + 1) * some, s * height : (s + 1) * height]
            for s in range(1, band_count)
        ]
        for h in range(HALVES)
    ]
    pieces[0] = [jnp.concatenate([piece, table], axis=1) for piece in pieces[0]]
    pieces = [spread([early] + pieces[h]) for h in range(HALVES)]
    early = [
        spread(delay_transform(me, matrices, height, pieces[h], EARLY_COST, h))
        for h in range(HALVES)
    ]
    mix, group = pair_weights(me, peer, parts * times, rows, height, [table] + pieces[0][1:])

    sums = jnp.zeros((GRP_DEV * band_count, sub), F32)
    by_time = [early[h][s] for s in range(band_count) for h in range(HALVES)]
    sums = pair_sums(mix, group, sums, [late])
    sums = pair_sums(mix, group, sums, by_time)
    sums = sums.reshape(band_count, GRP_DEV, sub)
    return interleave(me, spread([sums[s] for s in range(band_count)]))


def solution(mesh):
    band_count = mesh.shape["band"]

    def whole(visibilities, send_order, channel_flags, group_ids, pair_list):
        full_width = visibilities.shape[3]
        matrices = jnp.asarray(class_matrices(full_width, band_count))
        window = jnp.asarray(taper_window(full_width))
        mapped = jax.shard_map(
            on_device,
            mesh=mesh,
            in_specs=(
                P(),
                P(),
                P("bl", None, None, "band"),
                P("bl", None),
                P(),
                P(("band", "bl")),
                P(("band", "bl"), None),
            ),
            out_specs=P(("band", "bl"), None),
            check_vma=False,
        )
        return mapped(
            matrices, window, visibilities, send_order, channel_flags, group_ids, pair_list
        )

    return whole
```

```python
import functools
import math

import jax
import jax.numpy as jnp
import ml_dtypes
import numpy as np
from jax import lax
from jax.experimental import pallas as pl
from jax.experimental.pallas import tpu as pltpu
from jax.sharding import PartitionSpec as P

GRP_DEV = 16
LANES = 128
LATE_COST = 10**9
EARLY_COST = 10**9
HALVES = 2
LOADS = 8
PAIR_ROWS = 2
BF16_PARTS = 3
EXTRA_ROWS = 16
HIGHEST = lax.Precision.HIGHEST
VMEM_LIMIT = 20 * 1024 * 1024
F32 = jnp.float32
BF16 = jnp.bfloat16
VMEM = pl.BlockSpec(memory_space=pltpu.VMEM)
SMEM = pl.BlockSpec(memory_space=pltpu.SMEM)
HBM = pl.BlockSpec(memory_space=pltpu.HBM)


def shifted(value, axis, steps):
    count = lax.axis_size(axis)
    pairs = [(source, (source + steps) % count) for source in range(count)]
    return lax.ppermute(value, axis, pairs)


def spread(pieces):
    return [pieces[0]] + [shifted(pieces[s], "band", s) for s in range(1, len(pieces))]


def cost(flops, bytes_accessed):
    return pl.CostEstimate(flops=flops, bytes_accessed=bytes_accessed, transcendentals=0)


def params(limit=VMEM_LIMIT):
    return pltpu.CompilerParams(vmem_limit_bytes=limit)


def class_matrices(full_width, classes):
    sub = full_width // classes
    channel = np.arange(sub)[None, :, None]
    delay = classes * np.arange(sub)[None, None, :] + np.arange(classes)[:, None, None]
    angle = (channel * delay % full_width) * (2.0 * math.pi / full_width)
    cosine, sine = np.cos(angle), np.sin(angle)
    upper = np.concatenate([cosine, -sine], axis=2)
    lower = np.concatenate([sine, cosine], axis=2)
    return np.concatenate([upper, lower], axis=1).astype(ml_dtypes.bfloat16)


def taper_window(full_width):
    angle = np.arange(full_width) * (2.0 * math.pi / full_width)
    window = (
        0.35875
        - 0.48829 * np.cos(angle)
        + 0.14128 * np.cos(2.0 * angle)
        - 0.01168 * np.cos(3.0 * angle)
    )
    return window.reshape(1, -1).astype(np.float32)


def tiles_of(ref, where, start, count, column):
    tiles = [ref[where, pl.ds((start + c) * column, column), :] for c in range(count)]
    return jnp.concatenate([t.reshape(-1, LANES) for t in tiles], axis=1)


def taper_kernel(times, parts, band_count, me_ref, order_ref, window_ref, flags_ref, vis_ref, *refs):
    early_ref, late_refs = refs[0], refs[1:-6]
    vis_buf, slab_ref, early_buf, late_buf, load_sems, sems = refs[-6:]
    slabs, rows, _ = slab_ref.shape
    chunks = load_sems.shape[0]
    height = rows // chunks
    loads = []
    for k in range(chunks):
        where = pl.ds(k * height * slabs, height * slabs)
        loads.append(
            pltpu.make_async_copy(vis_ref.at[where, :], vis_buf.at[where, :], load_sems.at[k])
        )
        loads[-1].start()
    blocks = early_buf.shape[0]
    count, halves = late_buf.shape[:2]
    column = rows // blocks
    peer = column // band_count
    tiles = slabs // times
    sub = tiles // parts * LANES
    me = me_ref[0]
    here = pl.ds(pl.multiple_of(me * sub, sub), sub)
    weight = window_ref[:, here] * flags_ref[:, here].astype(F32)
    weight = jnp.concatenate([weight] * parts, axis=1)
    order = jnp.transpose(jnp.broadcast_to(order_ref[...].astype(F32), (LANES, rows)))
    if peer % 8 == 0:
        order = order.reshape(band_count, blocks, peer, LANES).transpose(1, 0, 2, 3)
        order = order.reshape(rows, LANES)
    lane = lax.broadcasted_iota(jnp.int32, (rows, LANES), 1)
    pick = [(lane + c == order.astype(jnp.int32)).astype(BF16) for c in range(0, rows, LANES)]
    pick = jnp.concatenate(pick, axis=1)
    for k, load in enumerate(loads):
        load.wait()
        block = vis_buf[k * height * slabs : (k + 1) * height * slabs, :]
        block = jnp.transpose(block.reshape(height, slabs, LANES), (1, 0, 2))
        slab_ref[:, k * height : (k + 1) * height, :] = block
    total = jnp.zeros((rows, LANES), F32)
    copies = []
    for half in (1, 0):
        for s in range(count):
            time = half * count + lax.rem(me + s, count)
            source = [
                slab_ref[(time * (tiles // parts) + tile) * parts + part]
                for part in range(parts)
                for tile in range(tiles // parts)
            ]
            moved = jnp.dot(pick, jnp.concatenate(source, axis=1), preferred_element_type=F32)
            tapered = (moved * weight).astype(BF16)
            squares = 0.0
            for c in range(tiles):
                tile = tapered[:, c * LANES : (c + 1) * LANES]
                wide = tile.astype(F32)
                squares = squares + wide * wide
                tile = tile.reshape(blocks, column, LANES)
                if half:
                    tile = tile.reshape(halves, blocks // halves, column, LANES)
                    late_buf[s, :, :, c * column : (c + 1) * column] = tile
                else:
                    start = (s * tiles + c) * column
                    early_buf[:, start : start + column] = tile
            total = total + squares
            if half:
                new = [
                    pltpu.make_async_copy(
                        late_buf.at[s, h], late_refs[h * count + s], sems.at[h * count + s]
                    )
                    for h in range(halves)
                ]
            else:
                where = pl.ds(s * tiles * column, tiles * column)
                new = [
                    pltpu.make_async_copy(
                        early_buf.at[:, where], early_ref.at[:, where], sems.at[halves * count + s]
                    )
                ]
            for copy in new:
                copy.start()
            copies += new
    energy = lax.dot_general(
        jnp.ones((EXTRA_ROWS, LANES), F32),
        total,
        (((1,), (1,)), ((), ())),
        precision=HIGHEST,
        preferred_element_type=F32,
    )
    row = lax.broadcasted_iota(jnp.int32, energy.shape, 0)
    rest, extra = energy, jnp.zeros_like(energy)
    for k in range(BF16_PARTS):
        part = rest.astype(BF16).astype(F32)
        extra = jnp.where(row == k, part, extra)
        rest = rest - part
    start = count * tiles * column
    for j in range(blocks):
        mine = extra[:, j * column : (j + 1) * column]
        mine = jnp.concatenate([mine, jnp.zeros((EXTRA_ROWS, LANES - column), F32)], axis=1)
        early_buf[j, start:] = mine.astype(BF16)
    where = pl.ds(start, EXTRA_ROWS)
    copy = pltpu.make_async_copy(
        early_buf.at[:, where], early_ref.at[:, where], sems.at[(halves + 1) * count]
    )
    copy.start()
    for copy in copies + [copy]:
        copy.wait()


def taper(band_count, blocks, me, order, window, flags, visibilities):
    rows, times, parts, sub = visibilities.shape
    count, lanes, tiles = times // 2, parts * sub, sub // LANES
    column = rows // blocks
    vis = visibilities.reshape(rows, times, parts, tiles, LANES).transpose(0, 1, 3, 2, 4)
    vis = vis.reshape(rows * times * tiles * parts, LANES)
    piece = (blocks // HALVES, parts * tiles * column, LANES)
    early = (blocks, count * parts * tiles * column + EXTRA_ROWS, LANES)
    return pl.pallas_call(
        functools.partial(taper_kernel, times, parts, band_count),
        out_shape=[jax.ShapeDtypeStruct(shape, BF16) for shape in [early] + [piece] * (HALVES * count)],
        in_specs=[SMEM, VMEM, VMEM, VMEM, HBM],
        out_specs=[HBM] * (1 + HALVES * count),
        scratch_shapes=[
            pltpu.VMEM(vis.shape, BF16),
            pltpu.VMEM((vis.shape[0] // rows, rows, LANES), BF16),
            pltpu.VMEM(early, BF16),
            pltpu.VMEM((count, HALVES) + piece, BF16),
            pltpu.SemaphoreType.DMA((LOADS,)),
            pltpu.SemaphoreType.DMA(((HALVES + 1) * count + 1,)),
        ],
        compiler_params=params(60 * 1024 * 1024),
        cost_estimate=cost(2 * times * rows * rows * lanes, 4 * times * rows * lanes),
        name="taper_rows",
    )(me, order, window, flags, vis)


def delay_kernel(half, me_ref, matrix_hbm, *refs):
    sources, outs = refs[:4], refs[4:8]
    x_refs, matrix_ref, mixed, out_buf, sems = refs[8:]
    blocks, height, _ = x_refs.shape[1:]
    lanes = mixed.shape[2]
    tiles = lanes // LANES
    column = height // tiles
    middle = lanes // 2
    me = me_ref[0]
    own = sources[0].at[pl.ds(half * blocks, blocks), pl.ds(0, height)]
    loads = [
        pltpu.make_async_copy(source, x_refs.at[s], sems.at[s])
        for s, source in enumerate([own] + [x.at[:, pl.ds(0, height)] for x in sources[1:]])
    ]
    loads.append(pltpu.make_async_copy(matrix_hbm, matrix_ref, sems.at[4]))
    for load in loads:
        load.start()
    for load in loads[:4]:
        load.wait()
    x = [tiles_of(x_refs.at[s], slice(None), 0, tiles, column).astype(F32) for s in range(4)]
    a, b, c, d = x[0] + x[2], x[0] - x[2], x[1] + x[3], x[1] - x[3]
    turned = jnp.concatenate([-d[:, middle:], d[:, :middle]], axis=1)
    for r, value in enumerate((a + c, b + turned, a - c, b - turned)):
        if r:
            turns = lax.rem(r * me, 4)
            real = jnp.where(turns == 0, 1.0, jnp.where(turns == 2, -1.0, 0.0)).astype(F32)
            imag = jnp.where(turns == 3, 1.0, jnp.where(turns == 1, -1.0, 0.0)).astype(F32)
            if r == 2:
                value = value * real
            else:
                other = jnp.concatenate([-value[:, middle:], value[:, :middle]], axis=1)
                value = value * real + other * imag
        mixed[r] = value.astype(BF16)
    loads[4].wait()
    stores = []
    for s in (1, 2, 3, 0):
        r = lax.rem(me + s, 4)
        out = jnp.dot(mixed[r], matrix_ref[r], preferred_element_type=F32).astype(BF16)
        for c in range(tiles):
            tile = out[:, c * LANES : (c + 1) * LANES].reshape(blocks, column, LANES)
            out_buf[s, :, c * column : (c + 1) * column] = tile
        stores.append(pltpu.make_async_copy(out_buf.at[s], outs[s], sems.at[5 + s]))
        stores[-1].start()
    for store in stores:
        store.wait()


def delay_transform(me, matrices, height, pieces, flops, half=0):
    _, lanes, _ = matrices.shape
    blocks = pieces[1].shape[0]
    piece = (blocks, height, LANES)
    rows = blocks * height * LANES // lanes
    return pl.pallas_call(
        functools.partial(delay_kernel, half),
        out_shape=[jax.ShapeDtypeStruct(piece, BF16)] * 4,
        in_specs=[SMEM] + [HBM] * 5,
        out_specs=[HBM] * 4,
        scratch_shapes=[
            pltpu.VMEM((4,) + piece, BF16),
            pltpu.VMEM(matrices.shape, BF16),
            pltpu.VMEM((4, rows, lanes), BF16),
            pltpu.VMEM((4,) + piece, BF16),
            pltpu.SemaphoreType.DMA((9,)),
        ],
        compiler_params=params(),
        cost_estimate=cost(flops, 16 * rows * lanes),
        name="delay_transform",
    )(me, matrices, *pieces)


def join_kernel(*refs):
    pieces, out_ref, buf, load_sems, store_sems = refs[:-4], *refs[-4:]
    count = len(pieces) // HALVES
    blocks, height, _ = pieces[0].shape
    loads, stores = [], []
    for k, piece in enumerate(pieces):
        loads.append(pltpu.make_async_copy(piece, buf.at[k], load_sems.at[k]))
        loads[-1].start()
    for k, load in enumerate(loads):
        load.wait()
        half, s = k // count, k % count
        where = out_ref.at[pl.ds(half * blocks, blocks), pl.ds(s * height, height)]
        stores.append(pltpu.make_async_copy(buf.at[k], where, store_sems.at[k]))
        stores[-1].start()
    for store in stores:
        store.wait()


def join(pieces):
    blocks, height, _ = pieces[0].shape
    out = (blocks * HALVES, height * (len(pieces) // HALVES), LANES)
    return pl.pallas_call(
        join_kernel,
        out_shape=jax.ShapeDtypeStruct(out, BF16),
        in_specs=[HBM] * len(pieces),
        out_specs=HBM,
        scratch_shapes=[
            pltpu.VMEM((len(pieces), blocks, height, LANES), BF16),
            pltpu.SemaphoreType.DMA((len(pieces),)),
            pltpu.SemaphoreType.DMA((len(pieces),)),
        ],
        compiler_params=params(),
        name="join_pieces",
    )(*pieces)


def pair_weights_kernel(peer, samples, height, me_ref, *refs):
    sources, mix_ref, group_ref, table_ref, sems = refs[:-4], *refs[-4:]
    band_count = len(sources)
    rows = mix_ref.shape[0]
    column = band_count * peer
    owned = rows // band_count
    me = me_ref[0]
    own = [sources[0]] + [x.at[:, pl.ds(height, EXTRA_ROWS)] for x in sources[1:]]
    loads = [pltpu.make_async_copy(x, table_ref.at[s], sems.at[s]) for s, x in enumerate(own)]
    for load in loads:
        load.start()
    for load in loads:
        load.wait()

    def line(table, start, count):
        return jnp.concatenate([table[start + k : start + k + 1] for k in range(count)], axis=1)

    energy, first, second, slot = 0.0, [], [], 0.0
    local = lax.broadcasted_iota(jnp.int32, (owned, rows), 0)
    place = lax.broadcasted_iota(jnp.int32, (owned, rows), 1)
    for s in range(band_count):
        owner = lax.rem(me + band_count - s, band_count)
        table = table_ref[s].astype(F32).reshape(-1, LANES)
        at = 0
        for _ in range(BF16_PARTS):
            energy = energy + line(table, at, rows // LANES)
            at += rows // LANES
        for out in (first, second):
            pair = line(table, at, PAIR_ROWS).astype(jnp.int32)
            at += PAIR_ROWS
            own = pair < owned
            pair = jnp.where(own, pair, pair - owned)
            source = jnp.where(own, owner, lax.rem(owner + band_count - 1, band_count))
            out.append(pair // peer * column + source * peer + pair % peer)
        groups = line(table, at, owned // LANES) + GRP_DEV * ((band_count - s) % band_count)
        here = local // peer * column + owner * peer + local % peer == place
        groups = jnp.broadcast_to(groups, (8, owned)).astype(BF16)
        slot = slot + jnp.dot(groups, here.astype(BF16), preferred_element_type=F32)
    energy = energy / samples + 1e-06
    place = lax.broadcasted_iota(jnp.int32, (rows, band_count * PAIR_ROWS * LANES), 0)
    contract_last = (((1,), (1,)), ((), ()))
    counts = lax.dot_general(
        (place == jnp.concatenate(first, axis=1)).astype(BF16),
        (place == jnp.concatenate(second, axis=1)).astype(BF16),
        contract_last,
        preferred_element_type=F32,
    )
    inverse = 1.0 / energy
    scale = inverse * jnp.sqrt(inverse)
    mix_ref[...] = (counts * scale).astype(BF16)
    partner = lax.dot_general(
        jnp.broadcast_to(inverse, (8, rows)),
        counts,
        contract_last,
        precision=HIGHEST,
        preferred_element_type=F32,
    )[0:1]
    slots = group_ref.shape[0]
    member = lax.broadcasted_iota(jnp.int32, (slots, rows), 0) == slot[0:1].astype(jnp.int32)
    denom = jnp.sum(jnp.where(member, inverse * partner, 0.0), axis=1, keepdims=True)
    group_ref[...] = jnp.where(member, scale, 0.0) / denom


def pair_weights(me, peer, samples, rows, height, tables):
    slots = GRP_DEV * len(tables)
    return pl.pallas_call(
        functools.partial(pair_weights_kernel, peer, samples, height),
        out_shape=[
            jax.ShapeDtypeStruct((rows, rows), BF16),
            jax.ShapeDtypeStruct((slots, rows), F32),
        ],
        in_specs=[SMEM] + [HBM] * len(tables),
        out_specs=[VMEM] * 2,
        scratch_shapes=[
            pltpu.VMEM((len(tables),) + tables[0].shape, BF16),
            pltpu.SemaphoreType.DMA((len(tables),)),
        ],
        compiler_params=params(),
        cost_estimate=cost(4 * rows * rows * rows, 4 * rows * rows),
        name="pair_weights",
    )(me, *tables)


def pair_kernel(by_hand, mix_ref, group_ref, before_ref, *refs):
    if by_hand:
        z_refs, out_ref, buf, sems = refs[:1], *refs[1:]
        height = buf.shape[2]
        loads = [
            pltpu.make_async_copy(z_refs[0].at[:, pl.ds(t * height, height)], buf.at[t], sems.at[t])
            for t in range(buf.shape[0])
        ]
        for load in loads:
            load.start()
        parts, count = 1, len(loads)
    else:
        z_refs, out_ref = refs[:-1], refs[-1]
        parts, count = HALVES, len(z_refs) // HALVES
    rows = mix_ref.shape[0]
    slots, half = out_ref.shape
    tiles = 2 * half // LANES
    column = rows // (parts * z_refs[0].shape[0])
    value = 0.0
    for t in range(count):
        if by_hand:
            loads[t].wait()
            window = tiles_of(buf.at[t], slice(None), 0, tiles, column)
        else:
            here = z_refs[t * parts : (t + 1) * parts]
            window = [tiles_of(ref, slice(None), 0, tiles, column) for ref in here]
            window = jnp.concatenate(window, axis=0)
        mixed = jnp.dot(mix_ref[...], window, preferred_element_type=F32)
        mixed = window.astype(F32) * mixed
        value = value + (mixed[:, :half] + mixed[:, half:])
    group = group_ref[...]
    group_high, value_high = group.astype(BF16), value.astype(BF16)
    group_low = (group - group_high.astype(F32)).astype(BF16)
    value_low = (value - value_high.astype(F32)).astype(BF16)
    both = jnp.concatenate([group_high, group_low], axis=0)
    part = jnp.dot(both, value_high, preferred_element_type=F32)
    part = part[:slots] + part[slots:]
    part = part + jnp.dot(group_high, value_low, preferred_element_type=F32)
    out_ref[...] = before_ref[...] + part


def pair_sums(mix, group, before, pieces):
    rows = mix.shape[1]
    half = before.shape[1]
    blocks, length, _ = pieces[0].shape
    by_hand = len(pieces) == 1
    scratch = []
    if by_hand:
        height = 2 * half // LANES * rows // blocks
        count = length // height
        scratch = [
            pltpu.VMEM((count, blocks, height, LANES), BF16),
            pltpu.SemaphoreType.DMA((count,)),
        ]
    else:
        count = len(pieces) // HALVES
    return pl.pallas_call(
        functools.partial(pair_kernel, by_hand),
        out_shape=jax.ShapeDtypeStruct(before.shape, F32),
        in_specs=[VMEM] * 3 + [HBM if by_hand else VMEM] * len(pieces),
        out_specs=VMEM,
        scratch_shapes=scratch,
        compiler_params=params(),
        cost_estimate=cost(4 * count * rows * rows * half, 4 * count * rows * half),
        name="pair_sums",
    )(mix, group, before, *pieces)


def interleave_kernel(me_ref, *refs):
    pieces, out_ref = refs[:-1], refs[-1]
    count = len(pieces)
    width = pieces[0].shape[1]
    me = me_ref[0]
    row = lax.broadcasted_iota(jnp.int32, (width, count * width), 0)
    column = lax.broadcasted_iota(jnp.int32, (width, count * width), 1)
    total = 0.0
    for s in range(count):
        r = lax.rem(me + count - s, count)
        pick = (column == row * count + r).astype(BF16)
        rest, parts = pieces[s][...], []
        for _ in range(BF16_PARTS):
            parts.append(rest.astype(BF16))
            rest = rest - parts[-1].astype(F32)
        parts = jnp.concatenate(parts, axis=0)
        total = total + jnp.dot(parts, pick, preferred_element_type=F32)
    groups = out_ref.shape[0]
    out_ref[...] = sum(total[k * groups : (k + 1) * groups] for k in range(BF16_PARTS))


def interleave(me, pieces):
    groups, width = pieces[0].shape
    return pl.pallas_call(
        interleave_kernel,
        out_shape=jax.ShapeDtypeStruct((groups, width * len(pieces)), F32),
        in_specs=[SMEM] + [VMEM] * len(pieces),
        out_specs=VMEM,
        compiler_params=params(),
        name="interleave_delays",
    )(me, *pieces)


def on_device(matrices, window, visibilities, send_order, channel_flags, group_ids, pair_list):
    band_count = lax.axis_size("band")
    block_count = lax.axis_size("bl")
    rows, times, parts, sub = visibilities.shape
    peer = rows // (band_count * block_count)
    column = band_count * peer
    height = parts * sub // LANES * column
    band = lax.axis_index("band").astype(jnp.int32)
    me = band.reshape(1)

    order = send_order
    if peer % 8:
        order = order.reshape(band_count, block_count, peer).transpose(1, 0, 2).reshape(1, rows)
    flags = channel_flags.reshape(1, -1)
    tables = jnp.concatenate([pair_list[:, 0], pair_list[:, 1], group_ids])
    tables = tables.astype(BF16).reshape(-1, LANES)
    early, *late = taper(band_count, block_count, me, order, window, flags, visibilities)

    early = lax.all_to_all(early, "bl", split_axis=0, concat_axis=0, tiled=True)
    late = [late[h * band_count : (h + 1) * band_count] for h in range(HALVES)]
    late = [spread(pieces) for pieces in late]
    late = [spread(delay_transform(me, matrices, height, pieces, LATE_COST)) for pieces in late]
    late = join([piece for pieces in late for piece in pieces])
    early, late = lax.optimization_barrier((early, late))
    late = lax.all_to_all(late, "bl", split_axis=0, concat_axis=0, tiled=True)

    some = block_count // HALVES
    energy = early[:, band_count * height :][:, :BF16_PARTS, :column]
    energy = energy.transpose(1, 0, 2).reshape(-1, LANES)
    table = jnp.concatenate([energy, tables], axis=0)
    table = jnp.pad(table, ((0, some * EXTRA_ROWS - table.shape[0]), (0, 0)))
    table = table.reshape(some, EXTRA_ROWS, LANES)
    pieces = [
        [
            early[h * some : (h + 1) * some, s * height : (s + 1) * height]
            for s in range(1, band_count)
        ]
        for h in range(HALVES)
    ]
    pieces[0] = [jnp.concatenate([piece, table], axis=1) for piece in pieces[0]]
    pieces = [spread([early] + pieces[h]) for h in range(HALVES)]
    early = [
        spread(delay_transform(me, matrices, height, pieces[h], EARLY_COST, h))
        for h in range(HALVES)
    ]
    mix, group = pair_weights(me, peer, parts * times, rows, height, [table] + pieces[0][1:])

    sums = jnp.zeros((GRP_DEV * band_count, sub), F32)
    by_time = [early[h][s] for s in range(band_count) for h in range(HALVES)]
    sums = pair_sums(mix, group, sums, [late])
    sums = pair_sums(mix, group, sums, by_time)
    sums = sums.reshape(band_count, GRP_DEV, sub)
    return interleave(me, spread([sums[s] for s in range(band_count)]))


def solution(mesh):
    band_count = mesh.shape["band"]

    def whole(visibilities, send_order, channel_flags, group_ids, pair_list):
        full_width = visibilities.shape[3]
        matrices = jnp.asarray(class_matrices(full_width, band_count))
        window = jnp.asarray(taper_window(full_width))
        mapped = jax.shard_map(
            on_device,
            mesh=mesh,
            in_specs=(
                P(),
                P(),
                P("bl", None, None, "band"),
                P("bl", None),
                P(),
                P(("band", "bl")),
                P(("band", "bl"), None),
            ),
            out_specs=P(("band", "bl"), None),
            check_vma=False,
        )
        return mapped(
            matrices, window, visibilities, send_order, channel_flags, group_ids, pair_list
        )

    return whole
```

```python
import functools
import math

import jax
import jax.numpy as jnp
import ml_dtypes
import numpy as np
from jax import lax
from jax.experimental import pallas as pl
from jax.experimental.pallas import tpu as pltpu
from jax.sharding import PartitionSpec as P

GRP_DEV = 16
LANES = 128
LATE_COST = 10**9
EARLY_COST = 10**9
HALVES = 2
LOADS = 16
PAIR_ROWS = 2
BF16_PARTS = 3
EXTRA_ROWS = 16
HIGHEST = lax.Precision.HIGHEST
VMEM_LIMIT = 20 * 1024 * 1024
F32 = jnp.float32
BF16 = jnp.bfloat16
VMEM = pl.BlockSpec(memory_space=pltpu.VMEM)
SMEM = pl.BlockSpec(memory_space=pltpu.SMEM)
HBM = pl.BlockSpec(memory_space=pltpu.HBM)


def shifted(value, axis, steps):
    count = lax.axis_size(axis)
    pairs = [(source, (source + steps) % count) for source in range(count)]
    return lax.ppermute(value, axis, pairs)


def spread(pieces):
    return [pieces[0]] + [shifted(pieces[s], "band", s) for s in range(1, len(pieces))]


def cost(flops, bytes_accessed):
    return pl.CostEstimate(flops=flops, bytes_accessed=bytes_accessed, transcendentals=0)


def params(limit=VMEM_LIMIT):
    return pltpu.CompilerParams(vmem_limit_bytes=limit)


def class_matrices(full_width, classes):
    sub = full_width // classes
    channel = np.arange(sub)[None, :, None]
    delay = classes * np.arange(sub)[None, None, :] + np.arange(classes)[:, None, None]
    angle = (channel * delay % full_width) * (2.0 * math.pi / full_width)
    cosine, sine = np.cos(angle), np.sin(angle)
    upper = np.concatenate([cosine, -sine], axis=2)
    lower = np.concatenate([sine, cosine], axis=2)
    return np.concatenate([upper, lower], axis=1).astype(ml_dtypes.bfloat16)


def taper_window(full_width):
    angle = np.arange(full_width) * (2.0 * math.pi / full_width)
    window = (
        0.35875
        - 0.48829 * np.cos(angle)
        + 0.14128 * np.cos(2.0 * angle)
        - 0.01168 * np.cos(3.0 * angle)
    )
    return window.reshape(1, -1).astype(np.float32)


def tiles_of(ref, where, start, count, column):
    tiles = [ref[where, pl.ds((start + c) * column, column), :] for c in range(count)]
    return jnp.concatenate([t.reshape(-1, LANES) for t in tiles], axis=1)


def taper_kernel(times, parts, band_count, me_ref, order_ref, window_ref, flags_ref, vis_ref, *refs):
    early_ref, late_refs = refs[0], refs[1:-6]
    vis_buf, slab_ref, early_buf, late_buf, load_sems, sems = refs[-6:]
    slabs, rows, _ = slab_ref.shape
    chunks = load_sems.shape[0]
    height = rows // chunks
    loads = []
    for k in range(chunks):
        where = pl.ds(k * height * slabs, height * slabs)
        loads.append(
            pltpu.make_async_copy(vis_ref.at[where, :], vis_buf.at[where, :], load_sems.at[k])
        )
        loads[-1].start()
    blocks = early_buf.shape[0]
    count, halves = late_buf.shape[:2]
    column = rows // blocks
    peer = column // band_count
    tiles = slabs // times
    sub = tiles // parts * LANES
    me = me_ref[0]
    here = pl.ds(pl.multiple_of(me * sub, sub), sub)
    weight = window_ref[:, here] * flags_ref[:, here].astype(F32)
    weight = jnp.concatenate([weight] * parts, axis=1)
    order = jnp.transpose(jnp.broadcast_to(order_ref[...].astype(F32), (LANES, rows)))
    if peer % 8 == 0:
        order = order.reshape(band_count, blocks, peer, LANES).transpose(1, 0, 2, 3)
        order = order.reshape(rows, LANES)
    lane = lax.broadcasted_iota(jnp.int32, (rows, LANES), 1)
    pick = [(lane + c == order.astype(jnp.int32)).astype(BF16) for c in range(0, rows, LANES)]
    pick = jnp.concatenate(pick, axis=1)
    for k, load in enumerate(loads):
        load.wait()
        block = vis_buf[k * height * slabs : (k + 1) * height * slabs, :]
        block = jnp.transpose(block.reshape(height, slabs, LANES), (1, 0, 2))
        slab_ref[:, k * height : (k + 1) * height, :] = block
    total = jnp.zeros((rows, LANES), F32)
    copies = []
    for half in (1, 0):
        for s in range(count):
            time = half * count + lax.rem(me + s, count)
            source = [
                slab_ref[(time * (tiles // parts) + tile) * parts + part]
                for part in range(parts)
                for tile in range(tiles // parts)
            ]
            moved = jnp.dot(pick, jnp.concatenate(source, axis=1), preferred_element_type=F32)
            tapered = (moved * weight).astype(BF16)
            for c in range(tiles):
                tile = tapered[:, c * LANES : (c + 1) * LANES]
                wide = tile.astype(F32)
                total = total + wide * wide
                tile = tile.reshape(blocks, column, LANES)
                if half:
                    tile = tile.reshape(halves, blocks // halves, column, LANES)
                    late_buf[s, :, :, c * column : (c + 1) * column] = tile
                else:
                    start = (s * tiles + c) * column
                    early_buf[:, start : start + column] = tile
            if half:
                new = [
                    pltpu.make_async_copy(
                        late_buf.at[s, h], late_refs[h * count + s], sems.at[h * count + s]
                    )
                    for h in range(halves)
                ]
            else:
                where = pl.ds(s * tiles * column, tiles * column)
                new = [
                    pltpu.make_async_copy(
                        early_buf.at[:, where], early_ref.at[:, where], sems.at[halves * count + s]
                    )
                ]
            for copy in new:
                copy.start()
            copies += new
    energy = lax.dot_general(
        jnp.ones((EXTRA_ROWS, LANES), F32),
        total,
        (((1,), (1,)), ((), ())),
        precision=HIGHEST,
        preferred_element_type=F32,
    )
    row = lax.broadcasted_iota(jnp.int32, energy.shape, 0)
    rest, extra = energy, jnp.zeros_like(energy)
    for k in range(BF16_PARTS):
        part = rest.astype(BF16).astype(F32)
        extra = jnp.where(row == k, part, extra)
        rest = rest - part
    start = count * tiles * column
    for j in range(blocks):
        mine = extra[:, j * column : (j + 1) * column]
        mine = jnp.concatenate([mine, jnp.zeros((EXTRA_ROWS, LANES - column), F32)], axis=1)
        early_buf[j, start:] = mine.astype(BF16)
    where = pl.ds(start, EXTRA_ROWS)
    copy = pltpu.make_async_copy(
        early_buf.at[:, where], early_ref.at[:, where], sems.at[(halves + 1) * count]
    )
    copy.start()
    for copy in copies + [copy]:
        copy.wait()


def taper(band_count, blocks, me, order, window, flags, visibilities):
    rows, times, parts, sub = visibilities.shape
    count, lanes, tiles = times // 2, parts * sub, sub // LANES
    column = rows // blocks
    vis = visibilities.reshape(rows, times, parts, tiles, LANES).transpose(0, 1, 3, 2, 4)
    vis = vis.reshape(rows * times * tiles * parts, LANES)
    piece = (blocks // HALVES, parts * tiles * column, LANES)
    early = (blocks, count * parts * tiles * column + EXTRA_ROWS, LANES)
    return pl.pallas_call(
        functools.partial(taper_kernel, times, parts, band_count),
        out_shape=[jax.ShapeDtypeStruct(shape, BF16) for shape in [early] + [piece] * (HALVES * count)],
        in_specs=[SMEM, VMEM, VMEM, VMEM, HBM],
        out_specs=[HBM] * (1 + HALVES * count),
        scratch_shapes=[
            pltpu.VMEM(vis.shape, BF16),
            pltpu.VMEM((vis.shape[0] // rows, rows, LANES), BF16),
            pltpu.VMEM(early, BF16),
            pltpu.VMEM((count, HALVES) + piece, BF16),
            pltpu.SemaphoreType.DMA((LOADS,)),
            pltpu.SemaphoreType.DMA(((HALVES + 1) * count + 1,)),
        ],
        compiler_params=params(60 * 1024 * 1024),
        cost_estimate=cost(2 * times * rows * rows * lanes, 4 * times * rows * lanes),
        name="taper_rows",
    )(me, order, window, flags, vis)


def delay_kernel(half, me_ref, matrix_hbm, *refs):
    sources, outs = refs[:4], refs[4:8]
    x_refs, matrix_ref, mixed, out_buf, sems = refs[8:]
    blocks, height, _ = x_refs.shape[1:]
    lanes = mixed.shape[2]
    tiles = lanes // LANES
    column = height // tiles
    middle = lanes // 2
    me = me_ref[0]
    own = sources[0].at[pl.ds(half * blocks, blocks), pl.ds(0, height)]
    loads = [
        pltpu.make_async_copy(source, x_refs.at[s], sems.at[s])
        for s, source in enumerate([own] + [x.at[:, pl.ds(0, height)] for x in sources[1:]])
    ]
    loads.append(pltpu.make_async_copy(matrix_hbm, matrix_ref, sems.at[4]))
    for load in loads:
        load.start()
    for load in loads[:4]:
        load.wait()
    x = [tiles_of(x_refs.at[s], slice(None), 0, tiles, column).astype(F32) for s in range(4)]
    a, b, c, d = x[0] + x[2], x[0] - x[2], x[1] + x[3], x[1] - x[3]
    turned = jnp.concatenate([-d[:, middle:], d[:, :middle]], axis=1)
    for r, value in enumerate((a + c, b + turned, a - c, b - turned)):
        if r:
            turns = lax.rem(r * me, 4)
            real = jnp.where(turns == 0, 1.0, jnp.where(turns == 2, -1.0, 0.0)).astype(F32)
            imag = jnp.where(turns == 3, 1.0, jnp.where(turns == 1, -1.0, 0.0)).astype(F32)
            if r == 2:
                value = value * real
            else:
                other = jnp.concatenate([-value[:, middle:], value[:, :middle]], axis=1)
                value = value * real + other * imag
        mixed[r] = value.astype(BF16)
    loads[4].wait()
    stores = []
    for s in (1, 2, 3, 0):
        r = lax.rem(me + s, 4)
        out = jnp.dot(mixed[r], matrix_ref[r], preferred_element_type=F32).astype(BF16)
        for c in range(tiles):
            tile = out[:, c * LANES : (c + 1) * LANES].reshape(blocks, column, LANES)
            out_buf[s, :, c * column : (c + 1) * column] = tile
        stores.append(pltpu.make_async_copy(out_buf.at[s], outs[s], sems.at[5 + s]))
        stores[-1].start()
    for store in stores:
        store.wait()


def delay_transform(me, matrices, height, pieces, flops, half=0):
    _, lanes, _ = matrices.shape
    blocks = pieces[1].shape[0]
    piece = (blocks, height, LANES)
    rows = blocks * height * LANES // lanes
    return pl.pallas_call(
        functools.partial(delay_kernel, half),
        out_shape=[jax.ShapeDtypeStruct(piece, BF16)] * 4,
        in_specs=[SMEM] + [HBM] * 5,
        out_specs=[HBM] * 4,
        scratch_shapes=[
            pltpu.VMEM((4,) + piece, BF16),
            pltpu.VMEM(matrices.shape, BF16),
            pltpu.VMEM((4, rows, lanes), BF16),
            pltpu.VMEM((4,) + piece, BF16),
            pltpu.SemaphoreType.DMA((9,)),
        ],
        compiler_params=params(),
        cost_estimate=cost(flops, 16 * rows * lanes),
        name="delay_transform",
    )(me, matrices, *pieces)


def join_kernel(*refs):
    pieces, out_ref, buf, load_sems, store_sems = refs[:-4], *refs[-4:]
    count = len(pieces) // HALVES
    blocks, height, _ = pieces[0].shape
    loads, stores = [], []
    for k, piece in enumerate(pieces):
        loads.append(pltpu.make_async_copy(piece, buf.at[k], load_sems.at[k]))
        loads[-1].start()
    for k, load in enumerate(loads):
        load.wait()
        half, s = k // count, k % count
        where = out_ref.at[pl.ds(half * blocks, blocks), pl.ds(s * height, height)]
        stores.append(pltpu.make_async_copy(buf.at[k], where, store_sems.at[k]))
        stores[-1].start()
    for store in stores:
        store.wait()


def join(pieces):
    blocks, height, _ = pieces[0].shape
    out = (blocks * HALVES, height * (len(pieces) // HALVES), LANES)
    return pl.pallas_call(
        join_kernel,
        out_shape=jax.ShapeDtypeStruct(out, BF16),
        in_specs=[HBM] * len(pieces),
        out_specs=HBM,
        scratch_shapes=[
            pltpu.VMEM((len(pieces), blocks, height, LANES), BF16),
            pltpu.SemaphoreType.DMA((len(pieces),)),
            pltpu.SemaphoreType.DMA((len(pieces),)),
        ],
        compiler_params=params(),
        name="join_pieces",
    )(*pieces)


def pair_weights_kernel(peer, samples, height, me_ref, *refs):
    sources, mix_ref, group_ref, table_ref, sems = refs[:-4], *refs[-4:]
    band_count = len(sources)
    rows = mix_ref.shape[0]
    column = band_count * peer
    owned = rows // band_count
    me = me_ref[0]
    own = [sources[0]] + [x.at[:, pl.ds(height, EXTRA_ROWS)] for x in sources[1:]]
    loads = [pltpu.make_async_copy(x, table_ref.at[s], sems.at[s]) for s, x in enumerate(own)]
    for load in loads:
        load.start()
    for load in loads:
        load.wait()

    def line(table, start, count):
        return jnp.concatenate([table[start + k : start + k + 1] for k in range(count)], axis=1)

    energy, first, second, slot = 0.0, [], [], 0.0
    local = lax.broadcasted_iota(jnp.int32, (owned, rows), 0)
    place = lax.broadcasted_iota(jnp.int32, (owned, rows), 1)
    for s in range(band_count):
        owner = lax.rem(me + band_count - s, band_count)
        table = table_ref[s].astype(F32).reshape(-1, LANES)
        at = 0
        for _ in range(BF16_PARTS):
            energy = energy + line(table, at, rows // LANES)
            at += rows // LANES
        for out in (first, second):
            pair = line(table, at, PAIR_ROWS).astype(jnp.int32)
            at += PAIR_ROWS
            own = pair < owned
            pair = jnp.where(own, pair, pair - owned)
            source = jnp.where(own, owner, lax.rem(owner + band_count - 1, band_count))
            out.append(pair // peer * column + source * peer + pair % peer)
        groups = line(table, at, owned // LANES) + GRP_DEV * ((band_count - s) % band_count)
        here = local // peer * column + owner * peer + local % peer == place
        groups = jnp.broadcast_to(groups, (8, owned)).astype(BF16)
        slot = slot + jnp.dot(groups, here.astype(BF16), preferred_element_type=F32)
    energy = energy / samples + 1e-06
    place = lax.broadcasted_iota(jnp.int32, (rows, band_count * PAIR_ROWS * LANES), 0)
    contract_last = (((1,), (1,)), ((), ()))
    counts = lax.dot_general(
        (place == jnp.concatenate(first, axis=1)).astype(BF16),
        (place == jnp.concatenate(second, axis=1)).astype(BF16),
        contract_last,
        preferred_element_type=F32,
    )
    inverse = 1.0 / energy
    scale = inverse * jnp.sqrt(inverse)
    mix_ref[...] = (counts * scale).astype(BF16)
    partner = lax.dot_general(
        jnp.broadcast_to(inverse, (8, rows)),
        counts,
        contract_last,
        precision=HIGHEST,
        preferred_element_type=F32,
    )[0:1]
    slots = group_ref.shape[0]
    member = lax.broadcasted_iota(jnp.int32, (slots, rows), 0) == slot[0:1].astype(jnp.int32)
    denom = jnp.sum(jnp.where(member, inverse * partner, 0.0), axis=1, keepdims=True)
    group_ref[...] = jnp.where(member, scale, 0.0) / denom


def pair_weights(me, peer, samples, rows, height, tables):
    slots = GRP_DEV * len(tables)
    return pl.pallas_call(
        functools.partial(pair_weights_kernel, peer, samples, height),
        out_shape=[
            jax.ShapeDtypeStruct((rows, rows), BF16),
            jax.ShapeDtypeStruct((slots, rows), F32),
        ],
        in_specs=[SMEM] + [HBM] * len(tables),
        out_specs=[VMEM] * 2,
        scratch_shapes=[
            pltpu.VMEM((len(tables),) + tables[0].shape, BF16),
            pltpu.SemaphoreType.DMA((len(tables),)),
        ],
        compiler_params=params(),
        cost_estimate=cost(4 * rows * rows * rows, 4 * rows * rows),
        name="pair_weights",
    )(me, *tables)


def pair_kernel(by_hand, mix_ref, group_ref, before_ref, *refs):
    if by_hand:
        z_refs, out_ref, buf, sems = refs[:1], *refs[1:]
        height = buf.shape[2]
        loads = [
            pltpu.make_async_copy(z_refs[0].at[:, pl.ds(t * height, height)], buf.at[t], sems.at[t])
            for t in range(buf.shape[0])
        ]
        for load in loads:
            load.start()
        parts, count = 1, len(loads)
    else:
        z_refs, out_ref = refs[:-1], refs[-1]
        parts, count = HALVES, len(z_refs) // HALVES
    rows = mix_ref.shape[0]
    slots, half = out_ref.shape
    tiles = 2 * half // LANES
    column = rows // (parts * z_refs[0].shape[0])
    value = 0.0
    for t in range(count):
        if by_hand:
            loads[t].wait()
            window = tiles_of(buf.at[t], slice(None), 0, tiles, column)
        else:
            here = z_refs[t * parts : (t + 1) * parts]
            window = [tiles_of(ref, slice(None), 0, tiles, column) for ref in here]
            window = jnp.concatenate(window, axis=0)
        mixed = jnp.dot(mix_ref[...], window, preferred_element_type=F32)
        mixed = window.astype(F32) * mixed
        value = value + (mixed[:, :half] + mixed[:, half:])
    group = group_ref[...]
    group_high, value_high = group.astype(BF16), value.astype(BF16)
    group_low = (group - group_high.astype(F32)).astype(BF16)
    value_low = (value - value_high.astype(F32)).astype(BF16)
    both = jnp.concatenate([group_high, group_low], axis=0)
    part = jnp.dot(both, value_high, preferred_element_type=F32)
    part = part[:slots] + part[slots:]
    part = part + jnp.dot(group_high, value_low, preferred_element_type=F32)
    out_ref[...] = before_ref[...] + part


def pair_sums(mix, group, before, pieces):
    rows = mix.shape[1]
    half = before.shape[1]
    blocks, length, _ = pieces[0].shape
    by_hand = len(pieces) == 1
    scratch = []
    if by_hand:
        height = 2 * half // LANES * rows // blocks
        count = length // height
        scratch = [
            pltpu.VMEM((count, blocks, height, LANES), BF16),
            pltpu.SemaphoreType.DMA((count,)),
        ]
    else:
        count = len(pieces) // HALVES
    return pl.pallas_call(
        functools.partial(pair_kernel, by_hand),
        out_shape=jax.ShapeDtypeStruct(before.shape, F32),
        in_specs=[VMEM] * 3 + [HBM if by_hand else VMEM] * len(pieces),
        out_specs=VMEM,
        scratch_shapes=scratch,
        compiler_params=params(),
        cost_estimate=cost(4 * count * rows * rows * half, 4 * count * rows * half),
        name="pair_sums",
    )(mix, group, before, *pieces)


def interleave_kernel(me_ref, *refs):
    pieces, out_ref = refs[:-1], refs[-1]
    count = len(pieces)
    width = pieces[0].shape[1]
    me = me_ref[0]
    row = lax.broadcasted_iota(jnp.int32, (width, count * width), 0)
    column = lax.broadcasted_iota(jnp.int32, (width, count * width), 1)
    total = 0.0
    for s in range(count):
        r = lax.rem(me + count - s, count)
        pick = (column == row * count + r).astype(BF16)
        rest, parts = pieces[s][...], []
        for _ in range(BF16_PARTS):
            parts.append(rest.astype(BF16))
            rest = rest - parts[-1].astype(F32)
        parts = jnp.concatenate(parts, axis=0)
        total = total + jnp.dot(parts, pick, preferred_element_type=F32)
    groups = out_ref.shape[0]
    out_ref[...] = sum(total[k * groups : (k + 1) * groups] for k in range(BF16_PARTS))


def interleave(me, pieces):
    groups, width = pieces[0].shape
    return pl.pallas_call(
        interleave_kernel,
        out_shape=jax.ShapeDtypeStruct((groups, width * len(pieces)), F32),
        in_specs=[SMEM] + [VMEM] * len(pieces),
        out_specs=VMEM,
        compiler_params=params(),
        name="interleave_delays",
    )(me, *pieces)


def on_device(matrices, window, visibilities, send_order, channel_flags, group_ids, pair_list):
    band_count = lax.axis_size("band")
    block_count = lax.axis_size("bl")
    rows, times, parts, sub = visibilities.shape
    peer = rows // (band_count * block_count)
    column = band_count * peer
    height = parts * sub // LANES * column
    band = lax.axis_index("band").astype(jnp.int32)
    me = band.reshape(1)

    order = send_order
    if peer % 8:
        order = order.reshape(band_count, block_count, peer).transpose(1, 0, 2).reshape(1, rows)
    flags = channel_flags.reshape(1, -1)
    tables = jnp.concatenate([pair_list[:, 0], pair_list[:, 1], group_ids])
    tables = tables.astype(BF16).reshape(-1, LANES)
    early, *late = taper(band_count, block_count, me, order, window, flags, visibilities)

    early = lax.all_to_all(early, "bl", split_axis=0, concat_axis=0, tiled=True)
    late = [late[h * band_count : (h + 1) * band_count] for h in range(HALVES)]
    late = [spread(pieces) for pieces in late]
    late = [spread(delay_transform(me, matrices, height, pieces, LATE_COST)) for pieces in late]
    late = join([piece for pieces in late for piece in pieces])
    early, late = lax.optimization_barrier((early, late))
    late = lax.all_to_all(late, "bl", split_axis=0, concat_axis=0, tiled=True)

    some = block_count // HALVES
    energy = early[:, band_count * height :][:, :BF16_PARTS, :column]
    energy = energy.transpose(1, 0, 2).reshape(-1, LANES)
    table = jnp.concatenate([energy, tables], axis=0)
    table = jnp.pad(table, ((0, some * EXTRA_ROWS - table.shape[0]), (0, 0)))
    table = table.reshape(some, EXTRA_ROWS, LANES)
    pieces = [
        [
            early[h * some : (h + 1) * some, s * height : (s + 1) * height]
            for s in range(1, band_count)
        ]
        for h in range(HALVES)
    ]
    pieces[0] = [jnp.concatenate([piece, table], axis=1) for piece in pieces[0]]
    pieces = [spread([early] + pieces[h]) for h in range(HALVES)]
    early = [
        spread(delay_transform(me, matrices, height, pieces[h], EARLY_COST, h))
        for h in range(HALVES)
    ]
    mix, group = pair_weights(me, peer, parts * times, rows, height, [table] + pieces[0][1:])

    sums = jnp.zeros((GRP_DEV * band_count, sub), F32)
    by_time = [early[h][s] for s in range(band_count) for h in range(HALVES)]
    sums = pair_sums(mix, group, sums, [late])
    sums = pair_sums(mix, group, sums, by_time)
    sums = sums.reshape(band_count, GRP_DEV, sub)
    return interleave(me, spread([sums[s] for s in range(band_count)]))


def solution(mesh):
    band_count = mesh.shape["band"]

    def whole(visibilities, send_order, channel_flags, group_ids, pair_list):
        full_width = visibilities.shape[3]
        matrices = jnp.asarray(class_matrices(full_width, band_count))
        window = jnp.asarray(taper_window(full_width))
        mapped = jax.shard_map(
            on_device,
            mesh=mesh,
            in_specs=(
                P(),
                P(),
                P("bl", None, None, "band"),
                P("bl", None),
                P(),
                P(("band", "bl")),
                P(("band", "bl"), None),
            ),
            out_specs=P(("band", "bl"), None),
            check_vma=False,
        )
        return mapped(
            matrices, window, visibilities, send_order, channel_flags, group_ids, pair_list
        )

    return whole
```
